256 devices in a mesh: rve: 32 (over x, z), slab: 8 (over y, core).
Axes of the slice: x: 4, y: 4, z: 8, core: 2. Of those that a mesh axis runs over, the one named last changes fastest.
Arguments:
- displacement: float32 [2, 8192, 128], P(None, ('rve', 'slab'))
- body_force: float32 [2, 8192, 128], P(None, ('rve', 'slab')), may hold values from -6 to 6
- assignment: int32 [4, 8192, 128], P(None, ('rve', 'slab')), may hold values from 0 to 31, as said below
- phases: int32 [32, 256, 256], P('rve', 'slab'), may hold values from 0 to 1
- flags: int32 [32, 256, 256], P('rve', 'slab'), may hold values 0 or 1
Outputs:
- correction: float32 [2, 8192, 128], P(None, ('rve', 'slab'))
- micro_strain: float32 [32, 3, 256, 256], P('rve', None, 'slab')
- homogenised: float32 [12, 32], replicated
The draws below stay inside these ranges and needn't reach their ends.
Inputs may be any that keep to these rules, and one draw needn't show every extreme that they name: `assignment`: every one of the 32 RVEs is named by at least one point.
All inputs are finite; a program needn't handle non-finite values. No bound on the sum of `flags` on one device may be relied on, other than what follows from the above.
Results may differ from the reference program's by a relative error of at most 0.0003.
Values sent between devices are 32-bit elements; how exact they have to be, the bound alone decides.
A program may use at most 64 MiB of HBM per device.

```python
import math
import jax
import jax.numpy as jnp
from jax import lax

G = 256
RVES = 32
EX = 32
EY = 128
ITERS = 2
CG_STEPS = 4
NX = 8192
N_SLAB = 8


def draw_displacement(key, part):
    key = jax.random.fold_in(key, 11)
    scale_key, offset_key, noise_key = jax.random.split(key, 3)
    column = jnp.arange(NX, dtype=jnp.float32)[None, :, None]
    row = jnp.arange(EY, dtype=jnp.float32)[None, None, :]
    period_x = 3.0 * EX * N_SLAB
    period_y = 1.0 * EY
    amplitude = jax.random.normal(scale_key, (2, 2), jnp.float32)
    ramp = 1.0 + 2.0 * column / NX
    noise = 0.5 * jax.random.normal(noise_key, (2, NX, EY), jnp.float32)
    offset = jax.random.uniform(offset_key, (2, 2), jnp.float32, 0.0, 2.0 * math.pi)
    wave_x = amplitude[:, 0, None, None] * (period_x / (2.0 * math.pi)) * jnp.sin(2.0 * math.pi * column / period_x + offset[:, 0, None, None])
    wave_y = amplitude[:, 1, None, None] * (period_y / (2.0 * math.pi)) * jnp.sin(2.0 * math.pi * row / period_y + offset[:, 1, None, None])
    return (ramp * (wave_x + wave_y) + noise).astype(jnp.float32)


def draw_assignment(key, part):
    key = jax.random.fold_in(key, 23)
    other_key, pick_key = jax.random.split(key)
    column = jnp.arange(NX, dtype=jnp.int32)[None, :, None]
    row = jnp.arange(EY, dtype=jnp.int32)[None, None, :]
    point = jnp.arange(4, dtype=jnp.int32)[:, None, None]
    home = column // (EX * N_SLAB)
    other = jax.random.randint(other_key, (4, NX, EY), 0, RVES, dtype=jnp.int32)
    pick = jax.random.randint(pick_key, (4, NX, EY), 0, 2, dtype=jnp.int32)
    forced = (point == 0) & (row == 0)
    return jnp.where((pick == 0) | forced, home, other).astype(jnp.int32)


def plant(array, rng, low, top_value):
    dims = array.shape
    place = [jax.random.randint(jax.random.fold_in(rng, axis), (), 0, dims[axis]) for axis in range(len(dims))]
    array = array.at[tuple(place)].set(low)
    longest = dims.index(max(dims))
    place[longest] = (place[longest] + 1) % dims[longest]
    return array.at[tuple(place)].set(top_value)


def block_levels(rng, shape, pieces, smallest, high):
    factor_of = 1.0
    for dim, shards_of in pieces:
        heights = jax.random.uniform(jax.random.fold_in(jax.random.fold_in(rng, 6), dim), (shards_of,), jnp.float32, smallest / len(pieces), high / len(pieces))
        factor_of = factor_of * jnp.repeat(jnp.exp(heights), shape[dim] // shards_of).reshape((-1,) + (1,) * (len(shape) - 1 - dim))
    return factor_of


def centred(rng, shape, scale, most, shards=(), held_as=jnp.bfloat16):
    values = scale * jax.random.normal(rng, shape, jnp.float32)
    if shards:
        values = values * block_levels(rng, shape, shards, -0.22, 0.18)
    return jnp.clip(values, -most, most).astype(held_as)


def setup_inputs(seed: int = 0) -> dict:
    key_list = jax.random.split(jax.random.key(seed), 6)
    return {
        "displacement": draw_displacement(jax.random.fold_in(key_list[5], 71), 0),
        "body_force": centred(key_list[1], (2, NX, EY), 1.0, 6.0, ((1, 256),), jnp.float32),
        "assignment": draw_assignment(jax.random.fold_in(key_list[5], 71), 0),
        "phases": plant(jax.random.randint(key_list[3], (RVES, G, G), 0, 2), jax.random.fold_in(key_list[3], 1), 0, 1).astype(jnp.int32),
        "flags": plant((jax.random.randint(key_list[4], (RVES, G, G), 0, 2) < 1).astype(jnp.int32), jax.random.fold_in(key_list[4], 1), 0, 1),
    }


MU_REF = 2.0
LAMBDA_REF = 2.0
COUPLE = (LAMBDA_REF + MU_REF) / (MU_REF * (LAMBDA_REF + 2.0 * MU_REF))
LOWER = 0.5 - 0.5 / math.sqrt(3.0)
UPPER = 0.5 + 0.5 / math.sqrt(3.0)
POINTS = ((LOWER, LOWER), (UPPER, LOWER), (LOWER, UPPER), (UPPER, UPPER))
WEIGHT = 0.25

def shape_slopes(point):
    coord_s, coord_t = point
    along_x = (-(1.0 - coord_t), 1.0 - coord_t, -coord_t, coord_t)
    along_y = (-(1.0 - coord_s), -coord_s, 1.0 - coord_s, coord_s)
    return (along_x, along_y)

def rows_up(field):
    return jnp.concatenate([field[..., 1:], jnp.zeros_like(field[..., :1])], -1)

def rows_down(field):
    return jnp.concatenate([jnp.zeros_like(field[..., :1]), field[..., :-1]], -1)

def corner_fields(field):
    right = jnp.concatenate([field[:, 1:], jnp.zeros_like(field[:, :1])], 1)
    return (field, right, rows_up(field), rows_up(right))

def strains_at(corners, point):
    along_x, along_y = shape_slopes(point)
    first = sum((along_x[a] * corners[a][0] for a in range(4)))
    second = sum((along_y[a] * corners[a][1] for a in range(4)))
    shear = sum((along_y[a] * corners[a][0] + along_x[a] * corners[a][1] for a in range(4)))
    return jnp.stack([first, second, shear])

def nodal_terms(stress, point):
    along_x, along_y = shape_slopes(point)
    terms = []
    for a in range(4):
        force_x = WEIGHT * (along_x[a] * stress[0] + along_y[a] * stress[2])
        force_y = WEIGHT * (along_y[a] * stress[1] + along_x[a] * stress[2])
        terms.append(jnp.stack([force_x, force_y]))
    return terms

def assemble(terms):
    gathered = terms[1] + rows_down(terms[3])
    shifted = jnp.concatenate([jnp.zeros_like(gathered[:, :1]), gathered[:, :-1]], 1)
    return terms[0] + rows_down(terms[2]) + shifted

def contract(tangent, vector):
    return jnp.stack([tangent[c] * vector[0] + tangent[3 + c] * vector[1] + tangent[6 + c] * vector[2] for c in range(3)])

def material(strain, bulk, shear, harden):
    volume = strain[0, 0] + strain[0, 1]
    normal_dev = 0.5 * (strain[0, 0] - strain[0, 1])
    shear_half = 0.5 * strain[0, 2]
    radius = 2.0 * normal_dev * normal_dev + 2.0 * shear_half * shear_half
    stiff = harden * radius
    factor = jnp.ones_like(radius)
    for turn in range(3):
        factor = factor - (factor + stiff * factor * factor * factor - 1.0) / (1.0 + 3.0 * stiff * factor * factor)
    slope = -harden * factor * factor * factor / (1.0 + 3.0 * stiff * factor * factor)
    stress = jnp.stack([bulk * volume + 2.0 * shear * factor * normal_dev, bulk * volume - 2.0 * shear * factor * normal_dev, 2.0 * shear * factor * shear_half])
    rest = strain[1:]
    d_volume = rest[:, 0] + rest[:, 1]
    d_normal = 0.5 * (rest[:, 0] - rest[:, 1])
    d_shear = 0.5 * rest[:, 2]
    d_factor = slope * (4.0 * normal_dev * d_normal + 4.0 * shear_half * d_shear)
    d_dev = 2.0 * shear * (factor * d_normal + d_factor * normal_dev)
    images = jnp.stack([bulk * d_volume + d_dev, bulk * d_volume - d_dev, 2.0 * shear * (factor * d_shear + d_factor * shear_half)], 1)
    return jnp.concatenate([stress[None], images], 0)

def frequencies(size):
    index = jnp.arange(size, dtype=jnp.int32)
    wrapped = jnp.where(index == size // 2, 0, index - size).astype(jnp.int32)
    return jnp.where(index < size // 2, index, wrapped).astype(jnp.float32)

def green_parts(freq_rows, freq_cols):
    square = freq_rows * freq_rows + freq_cols * freq_cols
    inverse = jnp.where(square > 0.0, 1.0 / jnp.maximum(square, 1.0), 0.0)
    return (freq_rows * freq_rows * inverse, freq_cols * freq_cols * inverse, freq_rows * freq_cols * inverse)

def green(first, second, mixed, part_11, part_22, part_12):
    total = part_11 * first + 2.0 * part_12 * mixed + part_22 * second
    out_11 = (part_11 * first + part_12 * mixed) / MU_REF - COUPLE * part_11 * total
    out_22 = (part_12 * mixed + part_22 * second) / MU_REF - COUPLE * part_22 * total
    out_12 = (part_12 * (first + second) + (part_11 + part_22) * mixed) / MU_REF - 2.0 * COUPLE * part_12 * total
    return (out_11, out_22, out_12)

def solve_cell(packed):
    mean_strain, phase, flag = packed
    bulk = jnp.where(phase == 1, 6.0, 2.0).astype(jnp.float32)
    shear = jnp.where(phase == 1, 3.0, 1.0).astype(jnp.float32)
    harden = flag.astype(jnp.float32) * jnp.where(phase == 1, 0.5, 2.0).astype(jnp.float32)
    part_11, part_22, part_12 = green_parts(frequencies(G)[:, None], frequencies(G)[None, :])
    start = jnp.concatenate([mean_strain[None], jnp.eye(3, dtype=jnp.float32)], 0)
    strain = jnp.broadcast_to(start[:, :, None, None], (4, 3, G, G))
    for step in range(ITERS):
        stress = material(strain, bulk, shear, harden)
        spectrum = jnp.fft.fft2(stress)
        out_11, out_22, out_12 = green(spectrum[:, 0], spectrum[:, 1], spectrum[:, 2], part_11, part_22, part_12)
        update = jnp.real(jnp.fft.ifft2(jnp.stack([out_11, out_22, out_12], 1)))
        strain = strain - update
    stress = material(strain, bulk, shear, harden)
    return (strain[0], lax.optimization_barrier(jnp.mean(stress, axis=(2, 3))).reshape(12))

def reference(displacement, body_force, assignment, phases, flags):
    corners = corner_fields(displacement)
    strains = [strains_at(corners, point) for point in POINTS]
    sums = jnp.zeros((RVES, 3), jnp.float32)
    counts = jnp.zeros((RVES,), jnp.float32)
    for index in range(4):
        labels = assignment[index].reshape(-1)
        sums = sums + jax.ops.segment_sum(strains[index].reshape(3, -1).T, labels, num_segments=RVES)
        counts = counts + jax.ops.segment_sum(jnp.ones(labels.shape, jnp.float32), labels, num_segments=RVES)
    means = (sums / counts[:, None]).T
    micro_strain, tables = lax.map(solve_cell, (means.T, phases, flags))
    homogenised = tables.T
    table = jnp.concatenate([homogenised, means], 0)
    totals = [jnp.zeros_like(displacement) for a in range(4)]
    for index, point in enumerate(POINTS):
        looked = jnp.take(table, assignment[index], axis=1)
        stress = looked[0:3] + contract(looked[3:12], strains[index] - looked[12:15])
        terms = nodal_terms(stress, point)
        totals = [totals[a] + terms[a] for a in range(4)]
    residual = body_force - assemble(totals)

    def stiffness(field):
        beside_all = corner_fields(field)
        parts = [jnp.zeros_like(field) for a in range(4)]
        for index, point in enumerate(POINTS):
            tangent = jnp.take(homogenised[3:12], assignment[index], axis=1)
            terms = nodal_terms(contract(tangent, strains_at(beside_all, point)), point)
            parts = [parts[a] + terms[a] for a in range(4)]
        return assemble(parts)
    correction = jnp.zeros_like(residual)
    direction = residual
    rho = jnp.sum(residual * residual)
    for step in range(CG_STEPS):
        image = stiffness(direction)
        alpha = rho / jnp.sum(direction * image)
        correction = correction + alpha * direction
        residual = residual - alpha * image
        fresh = jnp.sum(residual * residual)
        direction = residual + fresh / rho * direction
        rho = fresh
    return (correction, micro_strain, homogenised)
```

```python
import math

import jax
import jax.numpy as jnp
import ml_dtypes
import numpy as np
from jax import lax
from jax.experimental import pallas as pl
from jax.experimental.pallas import tpu as pltpu
from jax.sharding import PartitionSpec as P

MESH = pl.DeviceIdType.MESH
F32 = jnp.float32
BF16 = jnp.bfloat16

GRID = 256
HALF = 128
GROUPS = 32
SLABS = 8
BLOCK = 32
EXT = 48
CG_STEPS = 4

MU_REF = 2.0
LAMBDA_REF = 2.0
COUPLE = (LAMBDA_REF + MU_REF) / (MU_REF * (LAMBDA_REF + 2.0 * MU_REF))
LOWER = 0.5 - 0.5 / math.sqrt(3.0)
UPPER = 0.5 + 0.5 / math.sqrt(3.0)
ENDS = (LOWER, UPPER)
WEIGHT = 0.25
RANGE = 0.5

PAIRS = [(i, j) for i in range(CG_STEPS) for j in range(i, CG_STEPS + 1)]


def transform_tables():
    n = GRID
    place = np.arange(n)
    rows = []
    for slot in range(n):
        if slot < HALF:
            scale = math.sqrt((1.0 if slot == 0 else 2.0) / n)
            rows.append(scale * np.cos(2.0 * np.pi * (slot * place % n) / n))
        elif slot == HALF:
            rows.append(math.sqrt(1.0 / n) * np.cos(np.pi * place))
        else:
            rows.append(math.sqrt(2.0 / n) * np.sin(2.0 * np.pi * ((slot - HALF) * place % n) / n))
    forward = np.stack(rows).astype(np.float32)
    tables = []
    for table in (forward, forward.T):
        high = table.astype(ml_dtypes.bfloat16)
        low = (table - high.astype(np.float32)).astype(ml_dtypes.bfloat16)
        tables += [high, low]
    return np.stack(tables)


def lane_iota(shape):
    return lax.broadcasted_iota(jnp.int32, shape, len(shape) - 1)


def rows_up(field):
    rolled = pltpu.roll(field, field.shape[1] - 1, 1)
    return jnp.where(lane_iota(field.shape) == field.shape[1] - 1, 0.0, rolled)


def rows_down(field):
    rolled = pltpu.roll(field, 1, 1)
    return jnp.where(lane_iota(field.shape) == 0, 0.0, rolled)


def columns_back(field):
    return pltpu.roll(field, field.shape[0] - 1, 0)


def columns_on(field):
    return pltpu.roll(field, 1, 0)


def split(value):
    high = value.astype(BF16)
    return high, (value - high.astype(F32)).astype(BF16)


def dot(left, right):
    return jnp.dot(left, right, preferred_element_type=F32)


def strain_parts(first, second, first_next, second_next):
    across_1 = first_next - first
    across_2 = second_next - second
    across_1_up, across_2_up = rows_up(across_1), rows_up(across_2)
    up_1, up_2 = rows_up(first) - first, rows_up(second) - second
    up_1_next = rows_up(first_next) - first_next
    up_2_next = rows_up(second_next) - second_next
    d1x = [(1.0 - t) * across_1 + t * across_1_up for t in ENDS]
    d2x = [(1.0 - t) * across_2 + t * across_2_up for t in ENDS]
    d1y = [(1.0 - s) * up_1 + s * up_1_next for s in ENDS]
    d2y = [(1.0 - s) * up_2 + s * up_2_next for s in ENDS]
    return d1x, d2y, d1y, d2x


def assemble(stress):
    by_t = lambda c, t: stress[2 * t][c] + stress[2 * t + 1][c]
    by_s = lambda c, s: stress[s][c] + stress[2 + s][c]

    def mixed(parts):
        low = sum(WEIGHT * (1.0 - ENDS[k]) * parts[k] for k in range(2))
        high = sum(WEIGHT * ENDS[k] * parts[k] for k in range(2))
        return low, high

    forces = []
    for normal_x, normal_y in ((0, 2), (2, 1)):
        low, high = mixed([by_t(normal_x, t) for t in range(2)])
        over_x = low + rows_down(high)
        low, high = mixed([by_s(normal_y, s) for s in range(2)])
        over_y = low + columns_on(high)
        forces.append(columns_on(over_x) - over_x + rows_down(over_y) - over_y)
    return forces


def law(strain, harden):
    volume = strain[0] + strain[1]
    normal = 0.5 * (strain[0] - strain[1])
    shear = 0.5 * strain[2]
    stiff = harden * (2.0 * normal * normal + 2.0 * shear * shear)
    factor = (1.0 + 2.0 * stiff) / (1.0 + 3.0 * stiff)
    for turn in range(2):
        square = stiff * factor * factor
        factor = (1.0 + 2.0 * square * factor) / (1.0 + 3.0 * square)
    square = factor * factor
    slope = -harden * square * factor / (1.0 + 3.0 * stiff * square)
    return volume, normal, shear, factor, slope


def stress_of(state, bulk, modulus):
    volume, normal, shear, factor, slope = state
    spread = 2.0 * modulus * factor
    return [bulk * volume + spread * normal, bulk * volume - spread * normal, spread * shear]


def image_of(state, bulk, modulus, rest):
    volume, normal, shear, factor, slope = state
    d_volume = rest[0] + rest[1]
    d_normal = 0.5 * (rest[0] - rest[1])
    d_shear = 0.5 * rest[2]
    d_factor = slope * (4.0 * normal * d_normal + 4.0 * shear * d_shear)
    d_dev = 2.0 * modulus * (factor * d_normal + d_factor * normal)
    return [
        bulk * d_volume + d_dev,
        bulk * d_volume - d_dev,
        2.0 * modulus * (factor * d_shear + d_factor * shear),
    ]


def green(first, second, mixed, part_11, part_22, cross):
    across = cross * mixed
    total = part_11 * first + 2.0 * across + part_22 * second
    out_11 = (part_11 * first + across) * (1.0 / MU_REF) - COUPLE * part_11 * total
    out_22 = (across + part_22 * second) * (1.0 / MU_REF) - COUPLE * part_22 * total
    out_12 = (cross * (first + second) + (part_11 + part_22) * mixed) * (
        1.0 / MU_REF
    ) - 2.0 * COUPLE * cross * total
    return out_11, out_22, out_12


def kernel(
    disp, body, assign, phase, flag, table_hbm,
    correction_out, strain_out, hom_out,
    table, pf, a1src, a1, nb, a2src, a2, c1src, c1, c2src, c2, d1src, d1, d2src, d2,
    halo_u, halo_f, halo_a,
    parts, labels, accs, green_tab, ph_f, hard_f, ind_h, mid_h, mid_l, spec, filt_h, filt_l,
    strains, last, basis, tangent,
    sem_table, send, recv, gather_recv, halo_recv,
):
    r = lax.axis_index("rve")
    s = lax.axis_index("slab")
    y, core = s // 2, s % 2
    half, lane_field = s // 4, s % 4
    before, after = lax.rem(r + GROUPS - 1, GROUPS), lax.rem(r + 1, GROUPS)
    left = (jnp.where(s == 0, before, r), lax.rem(s + SLABS - 1, SLABS))
    right = (jnp.where(s == SLABS - 1, after, r), lax.rem(s + 1, SLABS))

    table_copy = pltpu.make_async_copy(table_hbm, table, sem_table)
    table_copy.start()

    barrier = pltpu.get_barrier_semaphore()

    def greet(device):
        pl.semaphore_signal(barrier, inc=1, device_id=device, device_id_type=MESH)

    for k in range(1, SLABS):
        greet((r, lax.rem(s + k, SLABS)))
    greet((after, 0))

    @pl.when(s == 0)
    def _():
        for k in range(SLABS):
            greet((before, k))

    for k in range(1, GROUPS):
        greet((lax.rem(r + k, GROUPS), s))

    pf[core, y, 0] = phase[...]
    pf[core, y, 1] = flag[...]

    def label_sums(rows, count):
        step = rows // 8

        def one(label, _):
            e = [parts[k, 0:rows, :] for k in range(8)]
            mask = [jnp.where(labels[p, 0:rows, :] == label.astype(F32), 1.0, 0.0) for p in range(4)]
            t_low, t_high = mask[0] + mask[1], mask[2] + mask[3]
            s_low, s_high = mask[0] + mask[2], mask[1] + mask[3]
            sums = [
                e[0] * t_low + e[1] * t_high,
                e[2] * s_low + e[3] * s_high,
                e[4] * s_low + e[5] * s_high + e[6] * t_low + e[7] * t_high,
            ]
            if count:
                sums.append(t_low + t_high)
            for c in range(len(sums)):
                accs[c, label] = jnp.sum(sums[c].reshape(step, 8, 128), axis=0)
            return 0

        lax.fori_loop(0, GROUPS, one, 0, unroll=4)
        if not count:
            accs[3] = jnp.zeros((GROUPS, 8, 128), F32)
        folded = jnp.sum(accs[...].reshape(4 * GROUPS, 8, 128), axis=1)
        ones = jnp.ones((8, 128), F32)
        return lax.dot_general(
            ones, folded, (((1,), (1,)), ((), ())),
            precision=lax.Precision.HIGHEST, preferred_element_type=F32,
        )[0:1, :]

    def keep_parts(fields, rows):
        d1x, d2y, d1y, d2x = strain_parts(*fields)
        for k, value in enumerate(d1x + d2y + d1y + d2x):
            parts[k, 0:rows, :] = value

    row_of = lax.broadcasted_iota(jnp.int32, (BLOCK, 128), 0)
    own = [disp[0], disp[1]]
    beside = [jnp.where(row_of == BLOCK - 1, 0.0, columns_back(u)) for u in own]
    keep_parts(own + beside, BLOCK)
    for p in range(4):
        labels[p] = assign[p].astype(F32)
    a1src[...] = jnp.concatenate(
        [label_sums(BLOCK, True), disp[0, 0:1, :], disp[1, 0:1, :]]
        + [labels[p, BLOCK - 1 : BLOCK, :] for p in range(4)]
        + [jnp.zeros((1, 128), F32)],
        axis=0,
    )
    a1[s] = a1src[...]

    def symbols(k, _):
        rows = pl.ds(pl.multiple_of(k * 32, 32), 32)
        row = lax.broadcasted_iota(jnp.int32, (32, GRID), 0) + k * 32
        lane = lax.broadcasted_iota(jnp.int32, (32, GRID), 1)
        k1 = lax.rem(row, HALF).astype(F32)
        k2 = lax.rem(lane, HALF).astype(F32)
        square = k1 * k1 + k2 * k2
        inverse = jnp.where(square > 0.0, 1.0 / jnp.maximum(square, 1.0), 0.0)
        sign = jnp.where((row < HALF) == (lane < HALF), -1.0, 1.0)
        green_tab[0, rows, :] = k1 * k1 * inverse
        green_tab[1, rows, :] = k2 * k2 * inverse
        green_tab[2, rows, :] = sign * k1 * k2 * inverse
        return 0

    lax.fori_loop(0, 8, symbols, 0)

    pl.semaphore_wait(barrier, SLABS - 1 + GROUPS - 1 + 1 + jnp.where(s == 0, SLABS, 0))

    def push(source, target, k, recv_sem, device):
        pltpu.make_async_remote_copy(
            source, target, send.at[k], recv_sem, device_id=device, device_id_type=MESH
        ).start()

    def drained(ref, sem):
        pltpu.make_async_copy(ref, ref, sem).wait()

    for k in range(1, SLABS):
        push(a1src, a1.at[s], 0, recv.at[0], (r, lax.rem(s + k, SLABS)))

    @pl.when(s == 0)
    def _():
        for k in range(SLABS):
            push(a1src, nb, 1, recv.at[1], (before, k))

    sibling = (r, y * 2 + 1 - core)
    for k in range(1, 4):
        push(pf.at[core, y], pf.at[core, y], 2, gather_recv.at[y], (r, lax.rem(y + k, 4) * 2 + core))
    push(pf.at[core, y], pf.at[core, y], 3, recv.at[2], sibling)

    for k, (own_ref, halo) in enumerate(((disp, halo_u), (body, halo_f), (assign, halo_a))):
        push(own_ref.at[:, pl.ds(0, 8), :], halo.at[1], 4 + 2 * k, halo_recv.at[k, 1], left)
        push(own_ref.at[:, pl.ds(BLOCK - 8, 8), :], halo.at[0], 5 + 2 * k, halo_recv.at[k, 0], right)

    drained(a1.at[pl.ds(0, SLABS - 1)], recv.at[0])
    drained(nb, recv.at[1])
    row8 = lax.broadcasted_iota(jnp.int32, (8, 128), 0)
    gathered = a1[...]
    at_end = jnp.where(r == GROUPS - 1, 0.0, 1.0)
    nxt = []
    for c in range(2):
        own_c = jnp.concatenate([gathered[k, 1 + c : 2 + c, :] for k in range(SLABS)], axis=0)
        nxt.append(jnp.where(row8 == 7, nb[1 + c : 2 + c, :] * at_end, columns_back(own_c)))
    zero8 = jnp.zeros((8, 128), F32)
    keep_parts([zero8, zero8] + nxt, 8)
    for p in range(4):
        labels[p, 0:8, :] = jnp.concatenate([gathered[k, 3 + p : 4 + p, :] for k in range(SLABS)], axis=0)
    a2src[...] = label_sums(8, False) + jnp.sum(gathered, axis=0)[0:1, :]
    a2[r] = a2src[...]
    for k in range(1, GROUPS):
        push(a2src, a2.at[r], 10, recv.at[3], (lax.rem(r + k, GROUPS), s))

    for k in range(1, 4):
        other = lax.rem(y + k, 4)
        drained(pf.at[core, other], gather_recv.at[other])
        push(pf.at[core, other], pf.at[core, other], 3, recv.at[2], sibling)
    drained(pf.at[1 - core], recv.at[2])

    for yy in range(4):
        for cc in range(2):
            rows = slice((yy * 2 + cc) * BLOCK, (yy * 2 + cc + 1) * BLOCK)
            here = pf[cc, yy, 0].astype(F32)
            active = pf[cc, yy, 1].astype(F32)
            ph_f[rows, :] = here
            hard_f[rows, :] = active * (2.0 - 1.5 * here)
            ind_h[0, rows, :] = here.astype(BF16)
            ind_h[1, rows, :] = active.astype(BF16)
            ind_h[2, rows, :] = (here * active).astype(BF16)

    table_copy.wait()

    def along_x(high, low, rows=slice(None), which=0):
        left_h, left_l = table[which, rows, :], table[which + 1, rows, :]
        return dot(left_h, high) + dot(left_h, low) + dot(left_l, high)

    def along_y(high, low, which):
        right_h, right_l = table[which], table[which + 1]
        return dot(high, right_h) + dot(high, right_l) + dot(low, right_h)

    for m in range(3):
        value = dot(ind_h[m], table[2]) + dot(ind_h[m], table[3])
        mid_h[m], mid_l[m] = split(value)
    for m in range(3):
        spec[m] = along_x(mid_h[m], mid_l[m])

    drained(a2.at[pl.ds(0, GROUPS - 1)], recv.at[3])
    totals = jnp.sum(a2[...], axis=0)
    lane1 = lane_iota((1, 128))
    picked = [
        jnp.sum(jnp.where(lane1 == 32 * c + r, totals, 0.0), axis=1, keepdims=True) for c in range(4)
    ]
    mean = [jnp.broadcast_to(picked[c] / picked[3], (8, 128)) for c in range(3)]
    unit = [jnp.where(lane_field == c, 1.0, 0.0) + jnp.where((lane_field == 3) & (c == 2), 1.0, 0.0) for c in range(3)]
    units = [jnp.full((8, 128), u, F32) for u in unit]

    kinds = {}
    for p in range(2):
        bulk, modulus = (6.0, 3.0) if p else (2.0, 1.0)
        for f in range(2):
            state = law(mean, (0.5 if p else 2.0) * f)
            kinds[p, f] = stress_of(state, bulk, modulus) + image_of(state, bulk, modulus, units)
    weights = []
    for k in range(6):
        base = kinds[0, 0][k]
        by_phase = kinds[1, 0][k] - base
        by_flag = kinds[0, 1][k] - base
        weights.append((by_phase, by_flag, kinds[1, 1][k] - base - by_phase - by_flag))

    def filter_all(load):
        def rows_of(k, _):
            for a in range(2):
                rows = pl.ds(pl.multiple_of(a * HALF + k * 16, 16), 16)
                swap_rows = pl.ds(pl.multiple_of((1 - a) * HALF + k * 16, 16), 16)
                for b in range(2):
                    lanes = slice(b * HALF, (b + 1) * HALF)
                    swap_lanes = slice((1 - b) * HALF, (2 - b) * HALF)
                    sym = [green_tab[i, rows, lanes] for i in range(3)]
                    firsts, seconds, mixeds = load(rows, lanes, swap_rows, swap_lanes)
                    for n in range(2):
                        out = green(firsts[n], seconds[n], mixeds[n], *sym)
                        for c in range(3):
                            rr, ll = (swap_rows, swap_lanes) if c == 2 else (rows, lanes)
                            high, low = split(out[c])
                            filt_h[3 * n + c, rr, ll] = high
                            filt_l[3 * n + c, rr, ll] = low
            return 0

        lax.fori_loop(0, 8, rows_of, 0)

    def wide(value):
        return jnp.concatenate([value, value], axis=0)

    wide_weights = [[wide(w) for w in three] for three in weights]

    def load_first(rows, lanes, swap_rows, swap_lanes):
        here = [spec[m, rows, lanes] for m in range(3)]
        there = [spec[m, swap_rows, swap_lanes] for m in range(3)]
        mix = lambda k, fields: sum(wide_weights[k][m] * fields[m] for m in range(3))
        return (
            [mix(0, here), mix(3, here)],
            [mix(1, here), mix(4, here)],
            [mix(2, there), mix(5, there)],
        )

    filter_all(load_first)

    start = mean + units
    for k in range(6):
        high, low = split(along_x(filt_h[k], filt_l[k], which=2))
        strains[k] = jnp.broadcast_to(start[k][0:1, 0:1], (GRID, GRID)) - along_y(high, low, 0)

    def material(k, _):
        rows = pl.ds(pl.multiple_of(k * 16, 16), 16)
        for b in range(2):
            lanes = slice(b * HALF, (b + 1) * HALF)
            here = ph_f[rows, lanes]
            state = law([strains[c, rows, lanes] for c in range(3)], hard_f[rows, lanes])
            bulk, modulus = 2.0 + 4.0 * here, 1.0 + 2.0 * here
            values = stress_of(state, bulk, modulus) + image_of(
                state, bulk, modulus, [strains[3 + c, rows, lanes] for c in range(3)]
            )
            for c in range(6):
                filt_h[c, rows, lanes], filt_l[c, rows, lanes] = split(values[c])
        return 0

    lax.fori_loop(0, 16, material, 0)
    for k in range(6):
        mid_h[k], mid_l[k] = split(along_y(filt_h[k], filt_l[k], 2))
    for k in range(6):
        spec[k] = along_x(mid_h[k], mid_l[k])

    def load_second(rows, lanes, swap_rows, swap_lanes):
        return (
            [spec[0, rows, lanes], spec[3, rows, lanes]],
            [spec[1, rows, lanes], spec[4, rows, lanes]],
            [spec[2, swap_rows, swap_lanes], spec[5, swap_rows, swap_lanes]],
        )

    filter_all(load_second)
    part = pl.ds(pl.multiple_of(half * HALF, HALF), HALF)
    for k in range(6):
        high, low = split(along_x(filt_h[k], filt_l[k], rows=part, which=2))
        last[k] = strains[k, part, :] - along_y(high, low, 0)

    def finish(k, sums):
        rows = pl.ds(pl.multiple_of(k * 16, 16), 16)
        full = pl.ds(pl.multiple_of(half * HALF + k * 16, 16), 16)
        sums = list(sums)
        for b in range(2):
            lanes = slice(b * HALF, (b + 1) * HALF)
            here = ph_f[full, lanes]
            state = law([last[c, rows, lanes] for c in range(3)], hard_f[full, lanes])
            bulk, modulus = 2.0 + 4.0 * here, 1.0 + 2.0 * here
            values = stress_of(state, bulk, modulus) + image_of(
                state, bulk, modulus, [last[3 + c, rows, lanes] for c in range(3)]
            )
            for c in range(6):
                sums[c] = sums[c] + values[c][0:8, :] + values[c][8:16, :]
        return tuple(sums)

    sums = lax.fori_loop(0, 8, finish, tuple(jnp.zeros((8, 128), F32) for c in range(6)))
    strain_out[0] = last[0:3, pl.ds(pl.multiple_of(lane_field * BLOCK, BLOCK), BLOCK), :]

    message = jnp.zeros((1, 128), F32)
    for c in range(3):
        stress_sum, image_sum = [
            jnp.sum(jnp.sum(sums[k], axis=0, keepdims=True), axis=1, keepdims=True) * (1.0 / (GRID * GRID))
            for k in (c, 3 + c)
        ]
        message = message + jnp.where((lane1 == c) & (lane_field == 0), stress_sum, 0.0)
        message = message + jnp.where((lane1 == 3 + 3 * lane_field + c) & (lane_field < 3), image_sum, 0.0)
        message = message + jnp.where((lane1 == 12 + c) & (s == 0), mean[c][0:1, :], 0.0)
    c1src[...] = message
    c1[s] = message
    for k in range(1, SLABS):
        push(c1src, c1.at[s], 11, recv.at[4], (r, lax.rem(s + k, SLABS)))

    for k, halo in enumerate((halo_u, halo_f, halo_a)):
        drained(halo.at[0], halo_recv.at[k, 0])
        drained(halo.at[1], halo_recv.at[k, 1])
    column = lax.broadcasted_iota(jnp.int32, (EXT, 128), 0) + ((r * SLABS + s) * BLOCK - 8)
    inside = (column >= 0) & (column < GROUPS * SLABS * BLOCK)

    def extended(halo, own_ref, c):
        return jnp.concatenate([halo[0, c], own_ref[c], halo[1, c]], axis=0)

    u = [jnp.where(inside, extended(halo_u, disp, c), 0.0) for c in range(2)]
    force = [extended(halo_f, body, c) for c in range(2)]
    index = [jnp.where(inside, extended(halo_a, assign, p), 127) for p in range(4)]
    u_parts = strain_parts(u[0], u[1], columns_back(u[0]), columns_back(u[1]))

    drained(c1.at[pl.ds(0, SLABS - 1)], recv.at[4])
    c2src[...] = jnp.sum(c1[...], axis=0)
    c2[r] = c2src[...]
    for k in range(1, GROUPS):
        push(c2src, c2.at[r], 12, recv.at[5], (lax.rem(r + k, GROUPS), s))
    drained(c2.at[pl.ds(0, GROUPS - 1)], recv.at[5])
    square = jnp.concatenate([c2[...].reshape(GROUPS, 128), jnp.zeros((128 - GROUPS, 128), F32)], axis=0)
    by_label = square.T[0:16, :]
    hom_out[...] = by_label[0:12, 0:GROUPS]
    rows = [by_label[k : k + 1, :] for k in range(15)]
    offset = [rows[c] - sum(rows[3 + 3 * j + c] * rows[12 + j] for j in range(3)) for c in range(3)]
    size = sum(jnp.abs(rows[k]) for k in range(3, 12))
    scale = RANGE * jnp.max(size, axis=1, keepdims=True)
    inverse_scale = 1.0 / scale

    def looked(row, p):
        return jnp.take_along_axis(jnp.broadcast_to(row, (EXT, 128)), index[p], axis=1, mode="promise_in_bounds")

    def point_strain(shapes, p):
        d1x, d2y, d1y, d2x = shapes
        sp, tp = p % 2, p // 2
        return d1x[tp], d2y[sp], d1y[sp] + d2x[tp]

    stress = []
    for p in range(4):
        strain = point_strain(u_parts, p)
        cs = [looked(rows[3 + k], p) for k in range(9)]
        for k in range(9):
            tangent[p, k] = cs[k]
        stress.append(
            [
                looked(offset[c], p) + cs[c] * strain[0] + cs[3 + c] * strain[1] + cs[6 + c] * strain[2]
                for c in range(3)
            ]
        )
    forces = assemble(stress)
    vector = [jnp.where(inside, force[c] - forces[c], 0.0) for c in range(2)]
    history = [vector]
    basis[0, 0], basis[0, 1] = vector[0][8:40], vector[1][8:40]

    def stiffness(field):
        shapes = strain_parts(field[0], field[1], columns_back(field[0]), columns_back(field[1]))
        result = []
        for p in range(4):
            strain = point_strain(shapes, p)
            result.append(
                [
                    tangent[p, c] * strain[0] + tangent[p, 3 + c] * strain[1] + tangent[p, 6 + c] * strain[2]
                    for c in range(3)
                ]
            )
        return assemble(result)

    for k in range(CG_STEPS):
        image = stiffness(history[k])
        shifted = [jnp.where(inside, image[c] * inverse_scale - history[k][c], 0.0) for c in range(2)]
        if k:
            shifted = [2.0 * shifted[c] - history[k - 1][c] for c in range(2)]
        history.append(shifted)
        basis[k + 1, 0], basis[k + 1, 1] = shifted[0][8:40], shifted[1][8:40]

    dots = []
    for i, j in PAIRS:
        product = basis[i, 0] * basis[j, 0] + basis[i, 1] * basis[j, 1]
        dots.append(jnp.sum(product.reshape(4, 8, 128), axis=(0, 1), keepdims=True).reshape(1, 128))
    dots += [jnp.zeros((1, 128), F32)] * (16 - len(dots))
    stacked = jnp.sum(jnp.concatenate(dots, axis=0), axis=1, keepdims=True)
    diagonal = lax.broadcasted_iota(jnp.int32, (16, 128), 0) == lane_iota((16, 128))
    d1src[...] = jnp.sum(jnp.where(diagonal, stacked, 0.0), axis=0, keepdims=True)
    d1[s] = d1src[...]
    for k in range(1, SLABS):
        push(d1src, d1.at[s], 13, recv.at[6], (r, lax.rem(s + k, SLABS)))
    drained(d1.at[pl.ds(0, SLABS - 1)], recv.at[6])
    d2src[...] = jnp.sum(d1[...], axis=0)
    d2[r] = d2src[...]
    for k in range(1, GROUPS):
        push(d2src, d2.at[r], 14, recv.at[7], (lax.rem(r + k, GROUPS), s))
    drained(d2.at[pl.ds(0, GROUPS - 1)], recv.at[7])
    gram_row = jnp.sum(d2[...], axis=0)
    gram = {}
    for k, (i, j) in enumerate(PAIRS):
        value = jnp.sum(jnp.where(lane1 == k, gram_row, 0.0), axis=1, keepdims=True)
        gram[i, j] = gram[j, i] = value

    def inner(one, two):
        return sum(one[i] * two[j] * gram[i, j] for i in range(len(one)) for j in range(len(two)))

    def apply(coefficients):
        n = len(coefficients)
        result = [scale * c for c in coefficients] + [0.0]
        for k in range(n):
            if k == 0:
                result[1] = result[1] + scale * coefficients[0]
            else:
                result[k + 1] = result[k + 1] + 0.5 * scale * coefficients[k]
                result[k - 1] = result[k - 1] + 0.5 * scale * coefficients[k]
        return result

    one = jnp.ones((1, 1), F32)
    direction, residual = [one], [one]
    answer = []
    rho = gram[0, 0]
    for step in range(CG_STEPS):
        image = apply(direction)
        alpha = rho / inner(direction, image)
        answer = [
            (answer[k] if k < len(answer) else 0.0) + alpha * direction[k] for k in range(len(direction))
        ]
        if step == CG_STEPS - 1:
            break
        residual = [
            (residual[k] if k < len(residual) else 0.0) - alpha * image[k] for k in range(len(image))
        ]
        fresh = inner(residual, residual)
        beta = fresh / rho
        direction = [
            residual[k] + (beta * direction[k] if k < len(direction) else 0.0) for k in range(len(residual))
        ]
        rho = fresh
    for c in range(2):
        correction_out[c] = sum(answer[k] * basis[k, c] for k in range(CG_STEPS))

    drained(a1.at[pl.ds(0, SLABS - 1)], send.at[0])

    @pl.when(s == 0)
    def _():
        drained(a1, send.at[1])

    drained(pf.at[0, pl.ds(0, 3)], send.at[2])
    drained(pf.at[0], send.at[3])
    for k, halo in enumerate((halo_u, halo_f, halo_a)):
        drained(halo.at[1], send.at[4 + 2 * k])
        drained(halo.at[0], send.at[5 + 2 * k])
    drained(a2.at[pl.ds(0, GROUPS - 1)], send.at[10])
    drained(c1.at[pl.ds(0, SLABS - 1)], send.at[11])
    drained(c2.at[pl.ds(0, GROUPS - 1)], send.at[12])
    drained(d1.at[pl.ds(0, SLABS - 1)], send.at[13])
    drained(d2.at[pl.ds(0, GROUPS - 1)], send.at[14])


def shards(displacement, body_force, assignment, phases, flags):
    tables = jnp.asarray(transform_tables())
    vmem = pl.BlockSpec(memory_space=pltpu.VMEM)
    row = lambda n: pltpu.VMEM((n, 1, 128), F32)
    one_row = pltpu.VMEM((1, 128), F32)
    square = (GRID, GRID)
    correction, strain, hom = pl.pallas_call(
        kernel,
        out_shape=(
            jax.ShapeDtypeStruct((2, BLOCK, 128), F32),
            jax.ShapeDtypeStruct((1, 3, BLOCK, GRID), F32),
            jax.ShapeDtypeStruct((12, GROUPS), F32),
        ),
        in_specs=[vmem] * 5 + [pl.BlockSpec(memory_space=pl.ANY)],
        out_specs=(vmem, vmem, vmem),
        scratch_shapes=[
            pltpu.VMEM((4,) + square, BF16),
            pltpu.VMEM((2, 4, 2, BLOCK, GRID), jnp.int32),
            pltpu.VMEM((8, 128), F32),
            pltpu.VMEM((SLABS, 8, 128), F32),
            pltpu.VMEM((8, 128), F32),
            one_row, row(GROUPS), one_row, row(SLABS), one_row, row(GROUPS),
            one_row, row(SLABS), one_row, row(GROUPS),
            pltpu.VMEM((2, 2, 8, 128), F32),
            pltpu.VMEM((2, 2, 8, 128), F32),
            pltpu.VMEM((2, 4, 8, 128), jnp.int32),
            pltpu.VMEM((8, BLOCK, 128), F32),
            pltpu.VMEM((4, BLOCK, 128), F32),
            pltpu.VMEM((4, GROUPS, 8, 128), F32),
            pltpu.VMEM((3,) + square, F32),
            pltpu.VMEM(square, F32),
            pltpu.VMEM(square, F32),
            pltpu.VMEM((3,) + square, BF16),
            pltpu.VMEM((6,) + square, BF16),
            pltpu.VMEM((6,) + square, BF16),
            pltpu.VMEM((6,) + square, F32),
            pltpu.VMEM((6,) + square, BF16),
            pltpu.VMEM((6,) + square, BF16),
            pltpu.VMEM((6,) + square, F32),
            pltpu.VMEM((6, HALF, GRID), F32),
            pltpu.VMEM((CG_STEPS + 1, 2, BLOCK, 128), F32),
            pltpu.VMEM((4, 9, EXT, 128), F32),
            pltpu.SemaphoreType.DMA,
            pltpu.SemaphoreType.DMA((15,)),
            pltpu.SemaphoreType.DMA((8,)),
            pltpu.SemaphoreType.DMA((4,)),
            pltpu.SemaphoreType.DMA((3, 2)),
        ],
        compiler_params=pltpu.CompilerParams(
            collective_id=0, has_side_effects=True, vmem_limit_bytes=48 * 1024 * 1024
        ),
        name="fe2_step",
    )(displacement, body_force, assignment, phases[0], flags[0], tables)
    return correction, strain, hom


def solution(mesh):
    return jax.shard_map(
        shards,
        mesh=mesh,
        in_specs=(
            P(None, ("rve", "slab"), None),
            P(None, ("rve", "slab"), None),
            P(None, ("rve", "slab"), None),
            P("rve", "slab", None),
            P("rve", "slab", None),
        ),
        out_specs=(P(None, ("rve", "slab"), None), P("rve", None, "slab", None), P()),
        check_vma=False,
    )
```

```python
import math

import jax
import jax.numpy as jnp
from jax import lax
from jax.experimental import pallas as pl
from jax.experimental.pallas import tpu as pltpu
from jax.sharding import PartitionSpec as P

MESH = pl.DeviceIdType.MESH
F32 = jnp.float32
BF16 = jnp.bfloat16

GRID = 256
HALF = 128
GROUPS = 32
SLABS = 8
BLOCK = 32
EXT = 48
CG_STEPS = 4

MU_REF = 2.0
LAMBDA_REF = 2.0
COUPLE = (LAMBDA_REF + MU_REF) / (MU_REF * (LAMBDA_REF + 2.0 * MU_REF))
LOWER = 0.5 - 0.5 / math.sqrt(3.0)
UPPER = 0.5 + 0.5 / math.sqrt(3.0)
ENDS = (LOWER, UPPER)
WEIGHT = 0.25
RANGE = 0.5

PAIRS = [(i, j) for i in range(CG_STEPS) for j in range(i, CG_STEPS + 1)]


def wave(slot, place):
    k = jnp.where(slot == HALF, HALF, lax.rem(slot, HALF))
    sine = slot > HALF
    turn = lax.bitwise_and(k * place + jnp.where(sine, 3 * GRID // 4, 0), GRID - 1)
    angle = (jnp.abs(turn - HALF) - GRID // 4).astype(F32) * (2.0 * math.pi / GRID)
    square = angle * angle
    value = 1.0 / 362880.0 - square * (1.0 / 39916800.0)
    for term in (1.0 / 5040.0, 1.0 / 120.0, 1.0 / 6.0, 1.0):
        value = term - square * value
    flat = (k == 0) | (k == HALF)
    return angle * value * jnp.where(flat, 1.0 / math.sqrt(GRID), math.sqrt(2.0 / GRID))


OFFSETS = sorted(
    ((dx, dz) for dx in range(4) for dz in range(8) if dx or dz),
    key=lambda o: -(min(o[0], 4 - o[0]) + min(o[1], 8 - o[1])),
)
NEAR = sorted(
    ((dy, dc) for dy in range(4) for dc in range(2) if dy or dc),
    key=lambda o: (-min(o[0], 4 - o[0]), -o[1]),
)


def lane_iota(shape):
    return lax.broadcasted_iota(jnp.int32, shape, len(shape) - 1)


def rows_up(field):
    rolled = pltpu.roll(field, field.shape[1] - 1, 1)
    return jnp.where(lane_iota(field.shape) == field.shape[1] - 1, 0.0, rolled)


def rows_down(field):
    rolled = pltpu.roll(field, 1, 1)
    return jnp.where(lane_iota(field.shape) == 0, 0.0, rolled)


def columns_back(field):
    return pltpu.roll(field, field.shape[0] - 1, 0)


def columns_on(field):
    return pltpu.roll(field, 1, 0)


def split(value):
    high = value.astype(BF16)
    return high, (value - high.astype(F32)).astype(BF16)


def dot(left, right):
    return jnp.dot(left, right, preferred_element_type=F32)


def strain_parts(first, second, first_next, second_next):
    across_1 = first_next - first
    across_2 = second_next - second
    across_1_up, across_2_up = rows_up(across_1), rows_up(across_2)
    up_1, up_2 = rows_up(first) - first, rows_up(second) - second
    up_1_next = rows_up(first_next) - first_next
    up_2_next = rows_up(second_next) - second_next
    d1x = [(1.0 - t) * across_1 + t * across_1_up for t in ENDS]
    d2x = [(1.0 - t) * across_2 + t * across_2_up for t in ENDS]
    d1y = [(1.0 - s) * up_1 + s * up_1_next for s in ENDS]
    d2y = [(1.0 - s) * up_2 + s * up_2_next for s in ENDS]
    return d1x, d2y, d1y, d2x


def assemble(stress):
    by_t = lambda c, t: stress[2 * t][c] + stress[2 * t + 1][c]
    by_s = lambda c, s: stress[s][c] + stress[2 + s][c]

    def mixed(parts):
        low = sum(WEIGHT * (1.0 - ENDS[k]) * parts[k] for k in range(2))
        high = sum(WEIGHT * ENDS[k] * parts[k] for k in range(2))
        return low, high

    forces = []
    for normal_x, normal_y in ((0, 2), (2, 1)):
        low, high = mixed([by_t(normal_x, t) for t in range(2)])
        over_x = low + rows_down(high)
        low, high = mixed([by_s(normal_y, s) for s in range(2)])
        over_y = low + columns_on(high)
        forces.append(columns_on(over_x) - over_x + rows_down(over_y) - over_y)
    return forces


def inverse(value):
    guess = pl.reciprocal(value, approx=True)
    return guess * (2.0 - value * guess)


def law(strain, harden):
    volume = strain[0] + strain[1]
    normal = 0.5 * (strain[0] - strain[1])
    shear = 0.5 * strain[2]
    stiff = harden * (2.0 * normal * normal + 2.0 * shear * shear)
    factor = (1.0 + 2.0 * stiff) * inverse(1.0 + 3.0 * stiff)
    for turn in range(2):
        square = stiff * factor * factor
        factor = (1.0 + 2.0 * square * factor) * inverse(1.0 + 3.0 * square)
    square = factor * factor
    slope = -harden * square * factor * inverse(1.0 + 3.0 * stiff * square)
    return volume, normal, shear, factor, slope


def stress_of(state, bulk, modulus):
    volume, normal, shear, factor, slope = state
    spread = 2.0 * modulus * factor
    return [bulk * volume + spread * normal, bulk * volume - spread * normal, spread * shear]


def image_of(state, bulk, modulus, rest):
    volume, normal, shear, factor, slope = state
    d_volume = rest[0] + rest[1]
    d_normal = 0.5 * (rest[0] - rest[1])
    d_shear = 0.5 * rest[2]
    d_factor = slope * (4.0 * normal * d_normal + 4.0 * shear * d_shear)
    d_dev = 2.0 * modulus * (factor * d_normal + d_factor * normal)
    return [
        bulk * d_volume + d_dev,
        bulk * d_volume - d_dev,
        2.0 * modulus * (factor * d_shear + d_factor * shear),
    ]


def green(first, second, mixed, part_11, part_22, cross):
    across = cross * mixed
    one, two = part_11 * first + across, part_22 * second + across
    total = (2.0 * MU_REF * COUPLE / 2.0) * (one + two)
    return (
        one - part_11 * total,
        two - part_22 * total,
        cross * (first + second - 2.0 * total) + (part_11 + part_22) * mixed,
    )


def kernel(
    disp_hbm, body_hbm, assign_hbm, phase_hbm, flag_hbm,
    correction_out, strain_0, strain_1, strain_2, hom_out,
    disp, body, assign, table, pf, a1src, a1, nb, a2src, a2, c1src, c1, c2src, c2, d1src, d1, d2src, d2,
    halo_u, halo_f, halo_a,
    parts, labels, accs, green_tab, ph_f, hard_f, ind_h, mid_h, mid_l, spec, filt_h, filt_l,
    strains, last, basis, tangent,
    load, send, recv, gather_recv, halo_recv,
):
    r = lax.axis_index("rve")
    s = lax.axis_index("slab")
    y, core = s // 2, s % 2
    half, lane_field = s // 4, s % 4
    before, after = lax.rem(r + GROUPS - 1, GROUPS), lax.rem(r + 1, GROUPS)
    peers = [(r, lax.rem(y + dy, 4) * 2 + (1 - core if dc else core)) for dy, dc in NEAR]
    gx, gz = r // 8, r % 8
    far = [(lax.rem(gx + dx, 4) * 8 + lax.rem(gz + dz, 8), s) for dx, dz in OFFSETS]
    left = (jnp.where(s == 0, before, r), lax.rem(s + SLABS - 1, SLABS))
    right = (jnp.where(s == SLABS - 1, after, r), lax.rem(s + 1, SLABS))

    loads = [
        pltpu.make_async_copy(source, target, load.at[k])
        for k, (source, target) in enumerate(
            (
                (disp_hbm, disp),
                (assign_hbm, assign),
                (phase_hbm.at[0], pf.at[core, y, 0]),
                (flag_hbm.at[0], pf.at[core, y, 1]),
                (body_hbm, body),
            )
        )
    ]
    for copy in loads:
        copy.start()

    barrier = pltpu.get_barrier_semaphore()

    def greet(device):
        pl.semaphore_signal(barrier, inc=1, device_id=device, device_id_type=MESH)

    for device in far:
        greet(device)
    for device in peers:
        greet(device)
    greet((after, 0))

    @pl.when(s == 0)
    def _():
        for k in range(SLABS):
            greet((before, k))

    def label_sums(rows, count):
        step = rows // 8

        def one(label, _):
            e = [parts[k, 0:rows, :] for k in range(8)]
            mask = [jnp.where(labels[p, 0:rows, :] == label.astype(F32), 1.0, 0.0) for p in range(4)]
            t_low, t_high = mask[0] + mask[1], mask[2] + mask[3]
            s_low, s_high = mask[0] + mask[2], mask[1] + mask[3]
            sums = [
                e[0] * t_low + e[1] * t_high,
                e[2] * s_low + e[3] * s_high,
                e[4] * s_low + e[5] * s_high + e[6] * t_low + e[7] * t_high,
            ]
            if count:
                sums.append(t_low + t_high)
            for c in range(len(sums)):
                accs[c, label] = jnp.sum(sums[c].reshape(step, 8, 128), axis=0)
            return 0

        lax.fori_loop(0, GROUPS, one, 0, unroll=GROUPS if rows == 8 else 4)
        if not count:
            accs[3] = jnp.zeros((GROUPS, 8, 128), F32)
        folded = jnp.sum(accs[...].reshape(4 * GROUPS, 8, 128), axis=1)
        ones = jnp.ones((8, 128), F32)
        return lax.dot_general(
            ones, folded, (((1,), (1,)), ((), ())),
            precision=lax.Precision.HIGHEST, preferred_element_type=F32,
        )[0:1, :]

    def keep_parts(fields, rows):
        d1x, d2y, d1y, d2x = strain_parts(*fields)
        for k, value in enumerate(d1x + d2y + d1y + d2x):
            parts[k, 0:rows, :] = value

    row_of = lax.broadcasted_iota(jnp.int32, (BLOCK, 128), 0)
    loads[0].wait()
    loads[1].wait()
    own = [disp[0], disp[1]]
    beside = [jnp.where(row_of == BLOCK - 1, 0.0, columns_back(u)) for u in own]
    keep_parts(own + beside, BLOCK)
    for p in range(4):
        labels[p] = assign[p].astype(F32)
    a1src[...] = jnp.concatenate(
        [label_sums(BLOCK, True), disp[0, 0:1, :], disp[1, 0:1, :]]
        + [labels[p, BLOCK - 1 : BLOCK, :] for p in range(4)]
        + [jnp.zeros((1, 128), F32)],
        axis=0,
    )
    a1[s] = a1src[...]

    def symbols(k, _):
        rows = pl.ds(pl.multiple_of(k * 32, 32), 32)
        row = lax.broadcasted_iota(jnp.int32, (32, GRID), 0) + k * 32
        lane = lax.broadcasted_iota(jnp.int32, (32, GRID), 1)
        k1 = lax.rem(row, HALF).astype(F32)
        k2 = lax.rem(lane, HALF).astype(F32)
        square = k1 * k1 + k2 * k2
        inverse = jnp.where(square > 0.0, 1.0 / jnp.maximum(square, 1.0), 0.0)
        sign = jnp.where((row < HALF) == (lane < HALF), -1.0, 1.0)
        green_tab[0, rows, :] = k1 * k1 * inverse
        green_tab[1, rows, :] = k2 * k2 * inverse
        green_tab[2, rows, :] = sign * k1 * k2 * inverse
        table[0, rows, :], table[1, rows, :] = split(wave(row, lane))
        table[2, rows, :], table[3, rows, :] = split(wave(lane, row))
        return 0

    lax.fori_loop(0, 8, symbols, 0)

    for copy in loads[2:5]:
        copy.wait()
    pl.semaphore_wait(barrier, SLABS - 1 + GROUPS - 1 + 1 + jnp.where(s == 0, SLABS, 0))

    def push(source, target, k, recv_sem, device):
        pltpu.make_async_remote_copy(
            source, target, send.at[k], recv_sem, device_id=device, device_id_type=MESH
        ).start()

    def drained(ref, sem):
        pltpu.make_async_copy(ref, ref, sem).wait()

    for device in peers:
        push(a1src, a1.at[s], 0, recv.at[0], device)

    @pl.when(s == 0)
    def _():
        for k in range(SLABS):
            push(a1src, nb, 1, recv.at[1], (before, k))

    sibling = (r, y * 2 + 1 - core)
    for k in range(1, 4):
        push(pf.at[core, y], pf.at[core, y], 2, gather_recv.at[y], (r, lax.rem(y + k, 4) * 2 + core))
    push(pf.at[core, y], pf.at[core, y], 3, recv.at[2], sibling)

    for k, (own_ref, halo) in enumerate(((disp, halo_u), (body, halo_f), (assign, halo_a))):
        push(own_ref.at[:, pl.ds(0, 8), :], halo.at[1], 4 + 2 * k, halo_recv.at[k, 1], left)
        push(own_ref.at[:, pl.ds(BLOCK - 8, 8), :], halo.at[0], 5 + 2 * k, halo_recv.at[k, 0], right)

    drained(a1.at[pl.ds(0, SLABS - 1)], recv.at[0])
    drained(nb, recv.at[1])
    row8 = lax.broadcasted_iota(jnp.int32, (8, 128), 0)
    gathered = a1[...]
    at_end = jnp.where(r == GROUPS - 1, 0.0, 1.0)
    nxt = []
    for c in range(2):
        own_c = jnp.concatenate([gathered[k, 1 + c : 2 + c, :] for k in range(SLABS)], axis=0)
        nxt.append(jnp.where(row8 == 7, nb[1 + c : 2 + c, :] * at_end, columns_back(own_c)))
    zero8 = jnp.zeros((8, 128), F32)
    keep_parts([zero8, zero8] + nxt, 8)
    for p in range(4):
        labels[p, 0:8, :] = jnp.concatenate([gathered[k, 3 + p : 4 + p, :] for k in range(SLABS)], axis=0)
    a2src[...] = label_sums(8, False) + jnp.sum(gathered, axis=0)[0:1, :]
    a2[r] = a2src[...]
    for device in far:
        push(a2src, a2.at[r], 10, recv.at[3], device)

    for k in range(1, 4):
        other = lax.rem(y + k, 4)
        drained(pf.at[core, other], gather_recv.at[other])
        push(pf.at[core, other], pf.at[core, other], 3, recv.at[2], sibling)
    drained(pf.at[1 - core], recv.at[2])

    for yy in range(4):
        for cc in range(2):
            rows = slice((yy * 2 + cc) * BLOCK, (yy * 2 + cc + 1) * BLOCK)
            here = pf[cc, yy, 0].astype(F32)
            active = pf[cc, yy, 1].astype(F32)
            ph_f[rows, :] = here
            hard_f[rows, :] = active * (2.0 - 1.5 * here)
            ind_h[0, rows, :] = here.astype(BF16)
            ind_h[1, rows, :] = active.astype(BF16)
            ind_h[2, rows, :] = (here * active).astype(BF16)


    def along_x(high, low, rows=slice(None), which=0):
        left_h, left_l = table[which, rows, :], table[which + 1, rows, :]
        return dot(left_h, high) + dot(left_h, low) + dot(left_l, high)

    def along_y(high, low, which):
        right_h, right_l = table[which], table[which + 1]
        return dot(high, right_h) + dot(high, right_l) + dot(low, right_h)

    for m in range(3):
        value = dot(ind_h[m], table[2]) + dot(ind_h[m], table[3])
        mid_h[m], mid_l[m] = split(value)
    for m in range(3):
        spec[m] = along_x(mid_h[m], mid_l[m])

    drained(a2.at[pl.ds(0, GROUPS - 1)], recv.at[3])
    totals = jnp.sum(a2[...], axis=0)
    lane1 = lane_iota((1, 128))
    picked = [
        jnp.sum(jnp.where(lane1 == 32 * c + r, totals, 0.0), axis=1, keepdims=True) for c in range(4)
    ]
    mean = [jnp.broadcast_to(picked[c] / picked[3], (8, 128)) for c in range(3)]
    unit = [jnp.where(lane_field == c, 1.0, 0.0) + jnp.where((lane_field == 3) & (c == 2), 1.0, 0.0) for c in range(3)]
    units = [jnp.full((8, 128), u, F32) for u in unit]

    kinds = {}
    for p in range(2):
        bulk, modulus = (6.0, 3.0) if p else (2.0, 1.0)
        for f in range(2):
            state = law(mean, (0.5 if p else 2.0) * f)
            kinds[p, f] = stress_of(state, bulk / MU_REF, modulus / MU_REF) + image_of(
                state, bulk / MU_REF, modulus / MU_REF, units
            )
    weights = []
    for k in range(6):
        base = kinds[0, 0][k]
        by_phase = kinds[1, 0][k] - base
        by_flag = kinds[0, 1][k] - base
        weights.append((by_phase, by_flag, kinds[1, 1][k] - base - by_phase - by_flag))

    def filter_all(load):
        def rows_of(k, _):
            for a in range(2):
                rows = pl.ds(pl.multiple_of(a * HALF + k * 16, 16), 16)
                swap_rows = pl.ds(pl.multiple_of((1 - a) * HALF + k * 16, 16), 16)
                for b in range(2):
                    lanes = slice(b * HALF, (b + 1) * HALF)
                    swap_lanes = slice((1 - b) * HALF, (2 - b) * HALF)
                    sym = [green_tab[i, rows, lanes] for i in range(3)]
                    firsts, seconds, mixeds = load(rows, lanes, swap_rows, swap_lanes)
                    for n in range(2):
                        out = green(firsts[n], seconds[n], mixeds[n], *sym)
                        for c in range(3):
                            rr, ll = (swap_rows, swap_lanes) if c == 2 else (rows, lanes)
                            high, low = split(out[c])
                            filt_h[3 * n + c, rr, ll] = high
                            filt_l[3 * n + c, rr, ll] = low
            return 0

        lax.fori_loop(0, 8, rows_of, 0, unroll=4)

    def wide(value):
        return jnp.concatenate([value, value], axis=0)

    wide_weights = [[wide(w) for w in three] for three in weights]

    def load_first(rows, lanes, swap_rows, swap_lanes):
        here = [spec[m, rows, lanes] for m in range(3)]
        there = [spec[m, swap_rows, swap_lanes] for m in range(3)]
        mix = lambda k, fields: sum(wide_weights[k][m] * fields[m] for m in range(3))
        return (
            [mix(0, here), mix(3, here)],
            [mix(1, here), mix(4, here)],
            [mix(2, there), mix(5, there)],
        )

    filter_all(load_first)

    start = mean + units
    for k in range(6):
        high, low = split(along_x(filt_h[k], filt_l[k], which=2))
        strains[k] = jnp.broadcast_to(start[k][0:1, 0:1], (GRID, GRID)) - along_y(high, low, 0)

    def material(k, _):
        rows = pl.ds(pl.multiple_of(k * 16, 16), 16)
        for b in range(2):
            lanes = slice(b * HALF, (b + 1) * HALF)
            here = ph_f[rows, lanes]
            state = law([strains[c, rows, lanes] for c in range(3)], hard_f[rows, lanes])
            bulk, modulus = 1.0 + 2.0 * here, 0.5 + here
            values = stress_of(state, bulk, modulus) + image_of(
                state, bulk, modulus, [strains[3 + c, rows, lanes] for c in range(3)]
            )
            for c in range(6):
                filt_h[c, rows, lanes], filt_l[c, rows, lanes] = split(values[c])
        return 0

    lax.fori_loop(0, 16, material, 0, unroll=4)
    for k in range(6):
        mid_h[k], mid_l[k] = split(along_y(filt_h[k], filt_l[k], 2))
    for k in range(6):
        spec[k] = along_x(mid_h[k], mid_l[k])

    def load_second(rows, lanes, swap_rows, swap_lanes):
        return (
            [spec[0, rows, lanes], spec[3, rows, lanes]],
            [spec[1, rows, lanes], spec[4, rows, lanes]],
            [spec[2, swap_rows, swap_lanes], spec[5, swap_rows, swap_lanes]],
        )

    filter_all(load_second)
    part = pl.ds(pl.multiple_of(half * HALF, HALF), HALF)
    for k in range(6):
        high, low = split(along_x(filt_h[k], filt_l[k], rows=part, which=2))
        last[k] = strains[k, part, :] - along_y(high, low, 0)

    def finish(k, sums):
        rows = pl.ds(pl.multiple_of(k * 16, 16), 16)
        full = pl.ds(pl.multiple_of(half * HALF + k * 16, 16), 16)
        sums = list(sums)
        for b in range(2):
            lanes = slice(b * HALF, (b + 1) * HALF)
            here = ph_f[full, lanes]
            state = law([last[c, rows, lanes] for c in range(3)], hard_f[full, lanes])
            bulk, modulus = 2.0 + 4.0 * here, 1.0 + 2.0 * here
            values = stress_of(state, bulk, modulus) + image_of(
                state, bulk, modulus, [last[3 + c, rows, lanes] for c in range(3)]
            )
            for c in range(6):
                sums[c] = sums[c] + values[c][0:8, :] + values[c][8:16, :]
        return tuple(sums)

    sums = lax.fori_loop(0, 8, finish, tuple(jnp.zeros((8, 128), F32) for c in range(6)), unroll=4)
    for c, strain_out in enumerate((strain_0, strain_1, strain_2)):
        strain_out[...] = last[c, pl.ds(pl.multiple_of(lane_field * BLOCK, BLOCK), BLOCK), :]

    message = jnp.zeros((1, 128), F32)
    for c in range(3):
        stress_sum, image_sum = [
            jnp.sum(jnp.sum(sums[k], axis=0, keepdims=True), axis=1, keepdims=True) * (1.0 / (GRID * GRID))
            for k in (c, 3 + c)
        ]
        message = message + jnp.where((lane1 == c) & (lane_field == 0), stress_sum, 0.0)
        message = message + jnp.where((lane1 == 3 + 3 * lane_field + c) & (lane_field < 3), image_sum, 0.0)
        message = message + jnp.where((lane1 == 12 + c) & (s == 0), mean[c][0:1, :], 0.0)
    c1src[...] = message
    c1[s] = message
    for device in peers:
        push(c1src, c1.at[s], 11, recv.at[4], device)

    for k, halo in enumerate((halo_u, halo_f, halo_a)):
        drained(halo.at[0], halo_recv.at[k, 0])
        drained(halo.at[1], halo_recv.at[k, 1])
    column = lax.broadcasted_iota(jnp.int32, (EXT, 128), 0) + ((r * SLABS + s) * BLOCK - 8)
    inside = (column >= 0) & (column < GROUPS * SLABS * BLOCK)

    def extended(halo, own_ref, c):
        return jnp.concatenate([halo[0, c], own_ref[c], halo[1, c]], axis=0)

    u = [jnp.where(inside, extended(halo_u, disp, c), 0.0) for c in range(2)]
    force = [extended(halo_f, body, c) for c in range(2)]
    index = [jnp.where(inside, extended(halo_a, assign, p), 127) for p in range(4)]
    u_parts = strain_parts(u[0], u[1], columns_back(u[0]), columns_back(u[1]))

    drained(c1.at[pl.ds(0, SLABS - 1)], recv.at[4])
    c2src[...] = jnp.sum(c1[...], axis=0)
    c2[r] = c2src[...]
    for device in far:
        push(c2src, c2.at[r], 12, recv.at[5], device)
    drained(c2.at[pl.ds(0, GROUPS - 1)], recv.at[5])
    square = jnp.concatenate([c2[...].reshape(GROUPS, 128), jnp.zeros((128 - GROUPS, 128), F32)], axis=0)
    by_label = square.T[0:16, :]
    hom_out[...] = by_label[0:12, 0:GROUPS]
    rows = [by_label[k : k + 1, :] for k in range(15)]
    offset = [rows[c] - sum(rows[3 + 3 * j + c] * rows[12 + j] for j in range(3)) for c in range(3)]
    size = sum(jnp.abs(rows[k]) for k in range(3, 12))
    scale = RANGE * jnp.max(size, axis=1, keepdims=True)
    inverse_scale = 1.0 / scale

    def looked(row, p):
        return jnp.take_along_axis(jnp.broadcast_to(row, (EXT, 128)), index[p], axis=1, mode="promise_in_bounds")

    def point_strain(shapes, p):
        d1x, d2y, d1y, d2x = shapes
        sp, tp = p % 2, p // 2
        return d1x[tp], d2y[sp], d1y[sp] + d2x[tp]

    stress = []
    for p in range(4):
        strain = point_strain(u_parts, p)
        cs = [looked(rows[3 + k], p) for k in range(9)]
        for k in range(9):
            tangent[p, k] = cs[k]
        stress.append(
            [
                looked(offset[c], p) + cs[c] * strain[0] + cs[3 + c] * strain[1] + cs[6 + c] * strain[2]
                for c in range(3)
            ]
        )
    forces = assemble(stress)
    vector = [jnp.where(inside, force[c] - forces[c], 0.0) for c in range(2)]
    history = [vector]
    basis[0, 0], basis[0, 1] = vector[0][8:40], vector[1][8:40]

    def stiffness(field):
        shapes = strain_parts(field[0], field[1], columns_back(field[0]), columns_back(field[1]))
        result = []
        for p in range(4):
            strain = point_strain(shapes, p)
            result.append(
                [
                    tangent[p, c] * strain[0] + tangent[p, 3 + c] * strain[1] + tangent[p, 6 + c] * strain[2]
                    for c in range(3)
                ]
            )
        return assemble(result)

    for k in range(CG_STEPS):
        image = stiffness(history[k])
        shifted = [jnp.where(inside, image[c] * inverse_scale - history[k][c], 0.0) for c in range(2)]
        if k:
            shifted = [2.0 * shifted[c] - history[k - 1][c] for c in range(2)]
        history.append(shifted)
        basis[k + 1, 0], basis[k + 1, 1] = shifted[0][8:40], shifted[1][8:40]

    dots = []
    for i, j in PAIRS:
        product = basis[i, 0] * basis[j, 0] + basis[i, 1] * basis[j, 1]
        dots.append(jnp.sum(product.reshape(4, 8, 128), axis=(0, 1), keepdims=True).reshape(1, 128))
    dots += [jnp.zeros((1, 128), F32)] * (16 - len(dots))
    stacked = jnp.sum(jnp.concatenate(dots, axis=0), axis=1, keepdims=True)
    diagonal = lax.broadcasted_iota(jnp.int32, (16, 128), 0) == lane_iota((16, 128))
    d1src[...] = jnp.sum(jnp.where(diagonal, stacked, 0.0), axis=0, keepdims=True)
    d1[s] = d1src[...]
    for device in peers:
        push(d1src, d1.at[s], 13, recv.at[6], device)
    drained(d1.at[pl.ds(0, SLABS - 1)], recv.at[6])
    d2src[...] = jnp.sum(d1[...], axis=0)
    d2[r] = d2src[...]
    for device in far:
        push(d2src, d2.at[r], 14, recv.at[7], device)
    drained(d2.at[pl.ds(0, GROUPS - 1)], recv.at[7])
    gram_row = jnp.sum(d2[...], axis=0)
    gram = {}
    for k, (i, j) in enumerate(PAIRS):
        value = jnp.sum(jnp.where(lane1 == k, gram_row, 0.0), axis=1, keepdims=True)
        gram[i, j] = gram[j, i] = value

    def inner(one, two):
        return sum(one[i] * two[j] * gram[i, j] for i in range(len(one)) for j in range(len(two)))

    def apply(coefficients):
        n = len(coefficients)
        result = [scale * c for c in coefficients] + [0.0]
        for k in range(n):
            if k == 0:
                result[1] = result[1] + scale * coefficients[0]
            else:
                result[k + 1] = result[k + 1] + 0.5 * scale * coefficients[k]
                result[k - 1] = result[k - 1] + 0.5 * scale * coefficients[k]
        return result

    one = jnp.ones((1, 1), F32)
    direction, residual = [one], [one]
    answer = []
    rho = gram[0, 0]
    for step in range(CG_STEPS):
        image = apply(direction)
        alpha = rho / inner(direction, image)
        answer = [
            (answer[k] if k < len(answer) else 0.0) + alpha * direction[k] for k in range(len(direction))
        ]
        if step == CG_STEPS - 1:
            break
        residual = [
            (residual[k] if k < len(residual) else 0.0) - alpha * image[k] for k in range(len(image))
        ]
        fresh = inner(residual, residual)
        beta = fresh / rho
        direction = [
            residual[k] + (beta * direction[k] if k < len(direction) else 0.0) for k in range(len(residual))
        ]
        rho = fresh
    for c in range(2):
        correction_out[c] = sum(answer[k] * basis[k, c] for k in range(CG_STEPS))

    drained(a1.at[pl.ds(0, SLABS - 1)], send.at[0])

    @pl.when(s == 0)
    def _():
        drained(a1, send.at[1])

    drained(pf.at[0, pl.ds(0, 3)], send.at[2])
    drained(pf.at[0], send.at[3])
    for k, halo in enumerate((halo_u, halo_f, halo_a)):
        drained(halo.at[1], send.at[4 + 2 * k])
        drained(halo.at[0], send.at[5 + 2 * k])
    drained(a2.at[pl.ds(0, GROUPS - 1)], send.at[10])
    drained(c1.at[pl.ds(0, SLABS - 1)], send.at[11])
    drained(c2.at[pl.ds(0, GROUPS - 1)], send.at[12])
    drained(d1.at[pl.ds(0, SLABS - 1)], send.at[13])
    drained(d2.at[pl.ds(0, GROUPS - 1)], send.at[14])


def write_kernel(one, two_a, two_b, two_c, three, one_out, two_out, three_out, sems):
    copies = [
        pltpu.make_async_copy(source, target, sems.at[k])
        for k, (source, target) in enumerate(
            (
                (one, one_out),
                (two_a, two_out.at[0, 0]),
                (two_b, two_out.at[0, 1]),
                (two_c, two_out.at[0, 2]),
                (three, three_out),
            )
        )
    ]
    for copy in copies:
        copy.start()
    for copy in copies:
        copy.wait()


def written(*values):
    return pl.pallas_call(
        write_kernel,
        out_shape=(
            jax.ShapeDtypeStruct((2, BLOCK, 128), F32),
            jax.ShapeDtypeStruct((1, 3, BLOCK, GRID), F32),
            jax.ShapeDtypeStruct((12, GROUPS), F32),
        ),
        in_specs=[pl.BlockSpec(memory_space=pl.ANY)] * 5,
        out_specs=(pl.BlockSpec(memory_space=pltpu.HBM),) * 3,
        scratch_shapes=[pltpu.SemaphoreType.DMA((5,))],
        compiler_params=pltpu.CompilerParams(vmem_limit_bytes=4 * 1024 * 1024),
        name="write_out",
    )(*values)


def shards(displacement, body_force, assignment, phases, flags):
    vmem = pl.BlockSpec(memory_space=pltpu.VMEM)
    row = lambda n: pltpu.VMEM((n, 1, 128), F32)
    one_row = pltpu.VMEM((1, 128), F32)
    square = (GRID, GRID)
    results = pl.pallas_call(
        kernel,
        out_shape=(
            jax.ShapeDtypeStruct((2, BLOCK, 128), F32),
            jax.ShapeDtypeStruct((BLOCK, GRID), F32),
            jax.ShapeDtypeStruct((BLOCK, GRID), F32),
            jax.ShapeDtypeStruct((BLOCK, GRID), F32),
            jax.ShapeDtypeStruct((12, GROUPS), F32),
        ),
        in_specs=[pl.BlockSpec(memory_space=pltpu.HBM)] * 5,
        out_specs=(vmem,) * 5,
        scratch_shapes=[
            pltpu.VMEM((2, BLOCK, 128), F32),
            pltpu.VMEM((2, BLOCK, 128), F32),
            pltpu.VMEM((4, BLOCK, 128), jnp.int32),
            pltpu.VMEM((4,) + square, BF16),
            pltpu.VMEM((2, 4, 2, BLOCK, GRID), jnp.int32),
            pltpu.VMEM((8, 128), F32),
            pltpu.VMEM((SLABS, 8, 128), F32),
            pltpu.VMEM((8, 128), F32),
            one_row, row(GROUPS), one_row, row(SLABS), one_row, row(GROUPS),
            one_row, row(SLABS), one_row, row(GROUPS),
            pltpu.VMEM((2, 2, 8, 128), F32),
            pltpu.VMEM((2, 2, 8, 128), F32),
            pltpu.VMEM((2, 4, 8, 128), jnp.int32),
            pltpu.VMEM((8, BLOCK, 128), F32),
            pltpu.VMEM((4, BLOCK, 128), F32),
            pltpu.VMEM((4, GROUPS, 8, 128), F32),
            pltpu.VMEM((3,) + square, F32),
            pltpu.VMEM(square, F32),
            pltpu.VMEM(square, F32),
            pltpu.VMEM((3,) + square, BF16),
            pltpu.VMEM((6,) + square, BF16),
            pltpu.VMEM((6,) + square, BF16),
            pltpu.VMEM((6,) + square, F32),
            pltpu.VMEM((6,) + square, BF16),
            pltpu.VMEM((6,) + square, BF16),
            pltpu.VMEM((6,) + square, F32),
            pltpu.VMEM((6, HALF, GRID), F32),
            pltpu.VMEM((CG_STEPS + 1, 2, BLOCK, 128), F32),
            pltpu.VMEM((4, 9, EXT, 128), F32),
            pltpu.SemaphoreType.DMA((5,)),
            pltpu.SemaphoreType.DMA((15,)),
            pltpu.SemaphoreType.DMA((8,)),
            pltpu.SemaphoreType.DMA((4,)),
            pltpu.SemaphoreType.DMA((3, 2)),
        ],
        compiler_params=pltpu.CompilerParams(
            collective_id=0, has_side_effects=True, vmem_limit_bytes=55080 * 1024
        ),
        name="fe2_step",
    )(displacement, body_force, assignment, phases, flags)
    return written(*results)


def solution(mesh):
    return jax.shard_map(
        shards,
        mesh=mesh,
        in_specs=(
            P(None, ("rve", "slab"), None),
            P(None, ("rve", "slab"), None),
            P(None, ("rve", "slab"), None),
            P("rve", "slab", None),
            P("rve", "slab", None),
        ),
        out_specs=(P(None, ("rve", "slab"), None), P("rve", None, "slab", None), P()),
        check_vma=False,
    )
```

```python
import math

import jax
import jax.numpy as jnp
from jax import lax
from jax.experimental import pallas as pl
from jax.experimental.pallas import tpu as pltpu
from jax.sharding import PartitionSpec as P

MESH = pl.DeviceIdType.MESH
F32 = jnp.float32
BF16 = jnp.bfloat16

GRID = 256
HALF = 128
GROUPS = 32
SLABS = 8
BLOCK = 32
EXT = 48
CG_STEPS = 4

MU_REF = 2.0
LAMBDA_REF = 2.0
COUPLE = (LAMBDA_REF + MU_REF) / (MU_REF * (LAMBDA_REF + 2.0 * MU_REF))
LOWER = 0.5 - 0.5 / math.sqrt(3.0)
UPPER = 0.5 + 0.5 / math.sqrt(3.0)
ENDS = (LOWER, UPPER)
WEIGHT = 0.25
RANGE = 0.5

PAIRS = [(i, j) for i in range(CG_STEPS) for j in range(i, CG_STEPS + 1)]


def wave(slot, place):
    k = jnp.where(slot == HALF, HALF, lax.rem(slot, HALF))
    sine = slot > HALF
    turn = lax.bitwise_and(k * place + jnp.where(sine, 3 * GRID // 4, 0), GRID - 1)
    angle = (jnp.abs(turn - HALF) - GRID // 4).astype(F32) * (2.0 * math.pi / GRID)
    square = angle * angle
    value = 1.0 / 362880.0 - square * (1.0 / 39916800.0)
    for term in (1.0 / 5040.0, 1.0 / 120.0, 1.0 / 6.0, 1.0):
        value = term - square * value
    flat = (k == 0) | (k == HALF)
    return angle * value * jnp.where(flat, 1.0 / math.sqrt(GRID), math.sqrt(2.0 / GRID))


OFFSETS = sorted(
    ((dx, dz) for dx in range(4) for dz in range(8) if dx or dz),
    key=lambda o: -(min(o[0], 4 - o[0]) + min(o[1], 8 - o[1])),
)
NEAR = sorted(
    ((dy, dc) for dy in range(4) for dc in range(2) if dy or dc),
    key=lambda o: (-min(o[0], 4 - o[0]), -o[1]),
)


def lane_iota(shape):
    return lax.broadcasted_iota(jnp.int32, shape, len(shape) - 1)


def rows_up(field):
    rolled = pltpu.roll(field, field.shape[1] - 1, 1)
    return jnp.where(lane_iota(field.shape) == field.shape[1] - 1, 0.0, rolled)


def rows_down(field):
    rolled = pltpu.roll(field, 1, 1)
    return jnp.where(lane_iota(field.shape) == 0, 0.0, rolled)


def columns_back(field):
    return pltpu.roll(field, field.shape[0] - 1, 0)


def columns_on(field):
    return pltpu.roll(field, 1, 0)


def split(value):
    high = value.astype(BF16)
    return high, (value - high.astype(F32)).astype(BF16)


def dot(left, right):
    return jnp.dot(left, right, preferred_element_type=F32)


def strain_parts(first, second, first_next, second_next):
    slopes = []
    for here, beside in ((first, first_next), (second, second_next)):
        above = rows_up(here)
        both = rows_up(beside)
        across, across_up = beside - here, both - above
        up, up_next = above - here, both - beside
        slopes.append(
            (
                [(1.0 - t) * across + t * across_up for t in ENDS],
                [(1.0 - s) * up + s * up_next for s in ENDS],
            )
        )
    return slopes[0][0], slopes[1][1], slopes[0][1], slopes[1][0]


def strain_parts_ext(field):
    slopes = []
    for here in field:
        above = rows_up(here)
        beside, both = columns_back(here), columns_back(above)
        across, across_up = beside - here, both - above
        up, up_next = above - here, both - beside
        slopes.append(
            (
                [(1.0 - t) * across + t * across_up for t in ENDS],
                [(1.0 - s) * up + s * up_next for s in ENDS],
            )
        )
    return slopes[0][0], slopes[1][1], slopes[0][1], slopes[1][0]


def assemble(stress):
    by_t = lambda c, t: stress[2 * t][c] + stress[2 * t + 1][c]
    by_s = lambda c, s: stress[s][c] + stress[2 + s][c]

    def mixed(parts):
        low = sum(WEIGHT * (1.0 - ENDS[k]) * parts[k] for k in range(2))
        high = sum(WEIGHT * ENDS[k] * parts[k] for k in range(2))
        return low, high

    forces = []
    for normal_x, normal_y in ((0, 2), (2, 1)):
        low_x, high_x = mixed([by_t(normal_x, t) for t in range(2)])
        low_y, high_y = mixed([by_s(normal_y, s) for s in range(2)])
        on = low_x - high_y + rows_down(high_x + high_y)
        forces.append(columns_on(on) - (low_x + low_y) + rows_down(low_y - high_x))
    return forces


def inverse(value):
    guess = pl.reciprocal(value, approx=True)
    return guess * (2.0 - value * guess)


def law(strain, harden):
    volume = strain[0] + strain[1]
    normal = 0.5 * (strain[0] - strain[1])
    shear = 0.5 * strain[2]
    stiff = harden * (2.0 * normal * normal + 2.0 * shear * shear)
    factor = (1.0 + 2.0 * stiff) * inverse(1.0 + 3.0 * stiff)
    for turn in range(2):
        square = stiff * factor * factor
        factor = (1.0 + 2.0 * square * factor) * inverse(1.0 + 3.0 * square)
    square = factor * factor
    slope = -harden * square * factor * inverse(1.0 + 3.0 * stiff * square)
    return volume, normal, shear, factor, slope


def stress_of(state, bulk, modulus):
    volume, normal, shear, factor, slope = state
    spread = 2.0 * modulus * factor
    return [bulk * volume + spread * normal, bulk * volume - spread * normal, spread * shear]


def image_of(state, bulk, modulus, rest):
    volume, normal, shear, factor, slope = state
    d_volume = rest[0] + rest[1]
    d_normal = 0.5 * (rest[0] - rest[1])
    d_shear = 0.5 * rest[2]
    d_factor = slope * (4.0 * normal * d_normal + 4.0 * shear * d_shear)
    d_dev = 2.0 * modulus * (factor * d_normal + d_factor * normal)
    return [
        bulk * d_volume + d_dev,
        bulk * d_volume - d_dev,
        2.0 * modulus * (factor * d_shear + d_factor * shear),
    ]


def green(first, second, mixed, part_11, part_22, cross):
    across = cross * mixed
    one, two = part_11 * first + across, part_22 * second + across
    total = (2.0 * MU_REF * COUPLE / 2.0) * (one + two)
    return (
        one - part_11 * total,
        two - part_22 * total,
        cross * (first + second - 2.0 * total) + (part_11 + part_22) * mixed,
    )


def kernel(
    disp_hbm, body_hbm, assign_hbm, phase_hbm, flag_hbm,
    correction_out, strain_0, strain_1, strain_2, hom_out,
    disp, body, assign, table, pf, a1src, a1, nb, a2src, a2, c1src, c1, c2src, c2, d1src, d1, d2src, d2,
    halo_u, halo_f, halo_a,
    parts, labels, accs, green_tab, ph_f, hard_f, mid_h, mid_l, spec, filt_h, filt_l,
    strains, last, basis, tangent,
    load, send, recv, gather_recv, halo_recv,
):
    r = lax.axis_index("rve")
    s = lax.axis_index("slab")
    y, core = s // 2, s % 2
    half, lane_field = s // 4, s % 4
    before, after = lax.rem(r + GROUPS - 1, GROUPS), lax.rem(r + 1, GROUPS)
    peers = [(r, lax.rem(y + dy, 4) * 2 + (1 - core if dc else core)) for dy, dc in NEAR]
    gx, gz = r // 8, r % 8
    far = [(lax.rem(gx + dx, 4) * 8 + lax.rem(gz + dz, 8), s) for dx, dz in OFFSETS]
    left = (jnp.where(s == 0, before, r), lax.rem(s + SLABS - 1, SLABS))
    right = (jnp.where(s == SLABS - 1, after, r), lax.rem(s + 1, SLABS))

    loads = [
        pltpu.make_async_copy(source, target, load.at[k])
        for k, (source, target) in enumerate(
            (
                (disp_hbm, disp),
                (assign_hbm, assign),
                (phase_hbm.at[0], pf.at[core, y, 0]),
                (flag_hbm.at[0], pf.at[core, y, 1]),
                (body_hbm, body),
            )
        )
    ]
    for copy in loads:
        copy.start()

    barrier = pltpu.get_barrier_semaphore()

    def greet(device):
        pl.semaphore_signal(barrier, inc=1, device_id=device, device_id_type=MESH)

    greet((after, 0))

    @pl.when(s == 0)
    def _():
        for k in range(SLABS):
            greet((before, k))

    for device in far:
        greet(device)
    for device in peers:
        greet(device)

    def label_sums(rows, count):
        step = rows // 8

        def one(label, _):
            e = [parts[k, 0:rows, :] for k in range(8)]
            mask = [jnp.where(labels[p, 0:rows, :] == label.astype(F32), 1.0, 0.0) for p in range(4)]
            t_low, t_high = mask[0] + mask[1], mask[2] + mask[3]
            s_low, s_high = mask[0] + mask[2], mask[1] + mask[3]
            sums = [
                e[0] * t_low + e[1] * t_high,
                e[2] * s_low + e[3] * s_high,
                e[4] * s_low + e[5] * s_high + e[6] * t_low + e[7] * t_high,
            ]
            if count:
                sums.append(t_low + t_high)
            for c in range(len(sums)):
                accs[c, label] = jnp.sum(sums[c].reshape(step, 8, 128), axis=0)
            return 0

        lax.fori_loop(0, GROUPS, one, 0, unroll=GROUPS if rows == 8 else 4)
        if not count:
            accs[3] = jnp.zeros((GROUPS, 8, 128), F32)
        folded = jnp.sum(accs[...].reshape(4 * GROUPS, 8, 128), axis=1)
        ones = jnp.ones((8, 128), F32)
        return lax.dot_general(
            ones, folded, (((1,), (1,)), ((), ())),
            precision=lax.Precision.HIGHEST, preferred_element_type=F32,
        )[0:1, :]

    def keep_parts(fields, rows):
        d1x, d2y, d1y, d2x = strain_parts(*fields)
        for k, value in enumerate(d1x + d2y + d1y + d2x):
            parts[k, 0:rows, :] = value

    row_of = lax.broadcasted_iota(jnp.int32, (BLOCK, 128), 0)
    loads[0].wait()
    loads[1].wait()
    own = [disp[0], disp[1]]
    beside = [jnp.where(row_of == BLOCK - 1, 0.0, columns_back(u)) for u in own]
    keep_parts(own + beside, BLOCK)
    for p in range(4):
        labels[p] = assign[p].astype(F32)
    a1src[...] = jnp.concatenate(
        [label_sums(BLOCK, True), disp[0, 0:1, :], disp[1, 0:1, :]]
        + [labels[p, BLOCK - 1 : BLOCK, :] for p in range(4)]
        + [jnp.zeros((1, 128), F32)],
        axis=0,
    )
    a1[s] = a1src[...]

    def symbols(k, _):
        rows = pl.ds(pl.multiple_of(k * 32, 32), 32)
        row = lax.broadcasted_iota(jnp.int32, (32, GRID), 0) + k * 32
        lane = lax.broadcasted_iota(jnp.int32, (32, GRID), 1)
        k1 = lax.rem(row, HALF).astype(F32)
        k2 = lax.rem(lane, HALF).astype(F32)
        square = k1 * k1 + k2 * k2
        inverse = jnp.where(square > 0.0, 1.0 / jnp.maximum(square, 1.0), 0.0)
        sign = jnp.where((row < HALF) == (lane < HALF), -1.0, 1.0)
        green_tab[0, rows, :] = k1 * k1 * inverse
        green_tab[1, rows, :] = k2 * k2 * inverse
        green_tab[2, rows, :] = sign * k1 * k2 * inverse
        table[0, rows, :], table[1, rows, :] = split(wave(row, lane))
        table[2, rows, :], table[3, rows, :] = split(wave(lane, row))
        return 0

    lax.fori_loop(0, 8, symbols, 0)

    for copy in loads[2:5]:
        copy.wait()
    pl.semaphore_wait(barrier, SLABS - 1 + GROUPS - 1 + 1 + jnp.where(s == 0, SLABS, 0))

    def push(source, target, k, recv_sem, device):
        pltpu.make_async_remote_copy(
            source, target, send.at[k], recv_sem, device_id=device, device_id_type=MESH
        ).start()

    def drained(ref, sem):
        pltpu.make_async_copy(ref, ref, sem).wait()

    @pl.when(s == 0)
    def _():
        for k in range(SLABS):
            push(a1src, nb, 1, recv.at[1], (before, k))

    for device in peers:
        push(a1src, a1.at[s], 0, recv.at[0], device)

    sibling = (r, y * 2 + 1 - core)
    for k in range(1, 4):
        push(pf.at[core, y], pf.at[core, y], 2, gather_recv.at[y], (r, lax.rem(y + k, 4) * 2 + core))
    push(pf.at[core, y], pf.at[core, y], 3, recv.at[2], sibling)

    for k, (own_ref, halo) in enumerate(((disp, halo_u), (body, halo_f), (assign, halo_a))):
        push(own_ref.at[:, pl.ds(0, 8), :], halo.at[1], 4 + 2 * k, halo_recv.at[k, 1], left)
        push(own_ref.at[:, pl.ds(BLOCK - 8, 8), :], halo.at[0], 5 + 2 * k, halo_recv.at[k, 0], right)

    drained(a1.at[pl.ds(0, SLABS - 1)], recv.at[0])
    drained(nb, recv.at[1])
    row8 = lax.broadcasted_iota(jnp.int32, (8, 128), 0)
    gathered = a1[...]
    at_end = jnp.where(r == GROUPS - 1, 0.0, 1.0)
    nxt = []
    for c in range(2):
        own_c = jnp.concatenate([gathered[k, 1 + c : 2 + c, :] for k in range(SLABS)], axis=0)
        nxt.append(jnp.where(row8 == 7, nb[1 + c : 2 + c, :] * at_end, columns_back(own_c)))
    zero8 = jnp.zeros((8, 128), F32)
    keep_parts([zero8, zero8] + nxt, 8)
    for p in range(4):
        labels[p, 0:8, :] = jnp.concatenate([gathered[k, 3 + p : 4 + p, :] for k in range(SLABS)], axis=0)
    a2src[...] = label_sums(8, False) + jnp.sum(gathered, axis=0)[0:1, :]
    a2[r] = a2src[...]
    for device in far:
        push(a2src, a2.at[r], 10, recv.at[3], device)

    def take_block(slab, chip):
        rows = pl.ds(pl.multiple_of((chip * 2 + slab) * BLOCK, BLOCK), BLOCK)
        here = pf[slab, chip, 0].astype(F32)
        active = pf[slab, chip, 1].astype(F32)
        ph_f[rows, :] = here
        hard_f[rows, :] = active * (2.0 - 1.5 * here)
        kinds_of = [here.astype(BF16), active.astype(BF16), (here * active).astype(BF16)]
        block = jnp.concatenate(kinds_of, axis=0)
        value = dot(block, table[2]) + dot(block, table[3])
        for m in range(3):
            part_h, part_l = split(value[m * BLOCK : (m + 1) * BLOCK])
            mid_h[m, rows, :] = part_h
            mid_l[m, rows, :] = part_l

    take_block(core, y)
    for k in range(1, 4):
        other = lax.rem(y + k, 4)
        drained(pf.at[core, other], gather_recv.at[other])
        push(pf.at[core, other], pf.at[core, other], 3, recv.at[2], sibling)
        take_block(core, other)
    drained(pf.at[1 - core], recv.at[2])
    for k in range(4):
        take_block(1 - core, k)

    def along_x(high, low, rows=slice(None), which=0):
        left_h, left_l = table[which, rows, :], table[which + 1, rows, :]
        return dot(left_h, high) + dot(left_h, low) + dot(left_l, high)

    def along_y(high, low, which):
        right_h, right_l = table[which], table[which + 1]
        return dot(high, right_h) + dot(high, right_l) + dot(low, right_h)

    for m in range(3):
        spec[m] = along_x(mid_h[m], mid_l[m])

    drained(a2.at[pl.ds(0, GROUPS - 1)], recv.at[3])
    totals = jnp.sum(a2[...], axis=0)
    lane1 = lane_iota((1, 128))
    picked = [
        jnp.sum(jnp.where(lane1 == 32 * c + r, totals, 0.0), axis=1, keepdims=True) for c in range(4)
    ]
    mean = [jnp.broadcast_to(picked[c] / picked[3], (8, 128)) for c in range(3)]
    unit = [jnp.where(lane_field == c, 1.0, 0.0) + jnp.where((lane_field == 3) & (c == 2), 1.0, 0.0) for c in range(3)]
    units = [jnp.full((8, 128), u, F32) for u in unit]

    kinds = {}
    for p in range(2):
        bulk, modulus = (6.0, 3.0) if p else (2.0, 1.0)
        for f in range(2):
            state = law(mean, (0.5 if p else 2.0) * f)
            kinds[p, f] = stress_of(state, bulk / MU_REF, modulus / MU_REF) + image_of(
                state, bulk / MU_REF, modulus / MU_REF, units
            )
    weights = []
    for k in range(6):
        base = kinds[0, 0][k]
        by_phase = kinds[1, 0][k] - base
        by_flag = kinds[0, 1][k] - base
        weights.append((by_phase, by_flag, kinds[1, 1][k] - base - by_phase - by_flag))

    def filter_pieces(load, n):
        def piece(k):
            for a in range(2):
                rows = slice(a * HALF + k * 16, a * HALF + k * 16 + 16)
                swap_rows = slice((1 - a) * HALF + k * 16, (1 - a) * HALF + k * 16 + 16)
                for b in range(2):
                    lanes = slice(b * HALF, (b + 1) * HALF)
                    swap_lanes = slice((1 - b) * HALF, (2 - b) * HALF)
                    sym = [green_tab[i, rows, lanes] for i in range(3)]
                    out = green(*load(n, rows, lanes, swap_rows, swap_lanes), *sym)
                    for c in range(3):
                        rr, ll = (swap_rows, swap_lanes) if c == 2 else (rows, lanes)
                        high, low = split(out[c])
                        filt_h[3 * n + c, rr, ll] = high
                        filt_l[3 * n + c, rr, ll] = low

        return [lambda k=k: piece(k) for k in range(8)]

    def together(first, second):
        turns = max(len(first), len(second))
        for k in range(turns):
            for pieces in (first, second):
                for j in range(k * len(pieces) // turns, (k + 1) * len(pieces) // turns):
                    pieces[j]()

    def wide(value):
        return jnp.concatenate([value, value], axis=0)

    wide_weights = [[wide(w) for w in three] for three in weights]

    def load_first(n, rows, lanes, swap_rows, swap_lanes):
        here = [spec[m, rows, lanes] for m in range(3)]
        there = [spec[m, swap_rows, swap_lanes] for m in range(3)]
        mix = lambda k, fields: sum(wide_weights[k][m] * fields[m] for m in range(3))
        return mix(3 * n, here), mix(3 * n + 1, here), mix(3 * n + 2, there)

    start = mean + units

    def invert_first(n):
        def one(k):
            high, low = split(along_x(filt_h[k], filt_l[k], which=2))
            strains[k] = jnp.broadcast_to(start[k][0:1, 0:1], (GRID, GRID)) - along_y(high, low, 0)

        return [lambda k=k: one(k) for k in range(3 * n, 3 * n + 3)]

    for piece in filter_pieces(load_first, 0):
        piece()
    together(filter_pieces(load_first, 1), invert_first(0))
    for piece in invert_first(1):
        piece()

    def material(k):
        rows = slice(k * 16, k * 16 + 16)
        for b in range(2):
            lanes = slice(b * HALF, (b + 1) * HALF)
            here = ph_f[rows, lanes]
            state = law([strains[c, rows, lanes] for c in range(3)], hard_f[rows, lanes])
            bulk, modulus = 1.0 + 2.0 * here, 0.5 + here
            values = stress_of(state, bulk, modulus) + image_of(
                state, bulk, modulus, [strains[3 + c, rows, lanes] for c in range(3)]
            )
            for c in range(6):
                filt_h[c, rows, lanes], filt_l[c, rows, lanes] = split(values[c])

    def forward_y(q):
        rows = slice(q * 64, q * 64 + 64)
        stacked = lambda ref: jnp.concatenate([ref[c, rows, :] for c in range(6)], axis=0)
        high, low = split(along_y(stacked(filt_h), stacked(filt_l), 2))
        for c in range(6):
            mid_h[c, rows, :] = high[c * 64 : c * 64 + 64]
            mid_l[c, rows, :] = low[c * 64 : c * 64 + 64]

    for q in range(5):
        pieces = [lambda k=k: material(k) for k in range(4 * q, 4 * q + 4)] if q < 4 else []
        together(pieces, [lambda: forward_y(q - 1)] if q else [])

    def load_second(n, rows, lanes, swap_rows, swap_lanes):
        return spec[3 * n, rows, lanes], spec[3 * n + 1, rows, lanes], spec[3 * n + 2, swap_rows, swap_lanes]

    part = pl.ds(pl.multiple_of(half * HALF, HALF), HALF)

    def forward_x(n):
        def one(k):
            spec[k] = along_x(mid_h[k], mid_l[k])

        return [lambda k=k: one(k) for k in range(3 * n, 3 * n + 3)]

    def invert_second(n):
        def one(k):
            high, low = split(along_x(filt_h[k], filt_l[k], rows=part, which=2))
            last[k] = strains[k, part, :] - along_y(high, low, 0)

        return [lambda k=k: one(k) for k in range(3 * n, 3 * n + 3)]

    for piece in forward_x(0):
        piece()
    together(filter_pieces(load_second, 0), forward_x(1))
    together(filter_pieces(load_second, 1), invert_second(0))
    for piece in invert_second(1):
        piece()

    def finish(k, sums):
        rows = pl.ds(pl.multiple_of(k * 16, 16), 16)
        full = pl.ds(pl.multiple_of(half * HALF + k * 16, 16), 16)
        sums = list(sums)
        for b in range(2):
            lanes = slice(b * HALF, (b + 1) * HALF)
            here = ph_f[full, lanes]
            state = law([last[c, rows, lanes] for c in range(3)], hard_f[full, lanes])
            bulk, modulus = 2.0 + 4.0 * here, 1.0 + 2.0 * here
            values = stress_of(state, bulk, modulus) + image_of(
                state, bulk, modulus, [last[3 + c, rows, lanes] for c in range(3)]
            )
            for c in range(6):
                sums[c] = sums[c] + values[c][0:8, :] + values[c][8:16, :]
        return tuple(sums)

    sums = lax.fori_loop(0, 8, finish, tuple(jnp.zeros((8, 128), F32) for c in range(6)), unroll=4)
    for c, strain_out in enumerate((strain_0, strain_1, strain_2)):
        strain_out[...] = last[c, pl.ds(pl.multiple_of(lane_field * BLOCK, BLOCK), BLOCK), :]

    message = jnp.zeros((1, 128), F32)
    for c in range(3):
        stress_sum, image_sum = [
            jnp.sum(jnp.sum(sums[k], axis=0, keepdims=True), axis=1, keepdims=True) * (1.0 / (GRID * GRID))
            for k in (c, 3 + c)
        ]
        message = message + jnp.where((lane1 == c) & (lane_field == 0), stress_sum, 0.0)
        message = message + jnp.where((lane1 == 3 + 3 * lane_field + c) & (lane_field < 3), image_sum, 0.0)
        message = message + jnp.where((lane1 == 12 + c) & (s == 0), mean[c][0:1, :], 0.0)
    c1src[...] = message
    c1[s] = message
    for device in peers:
        push(c1src, c1.at[s], 11, recv.at[4], device)

    for k, halo in enumerate((halo_u, halo_f, halo_a)):
        drained(halo.at[0], halo_recv.at[k, 0])
        drained(halo.at[1], halo_recv.at[k, 1])
    column = lax.broadcasted_iota(jnp.int32, (EXT, 128), 0) + ((r * SLABS + s) * BLOCK - 8)
    inside = (column >= 0) & (column < GROUPS * SLABS * BLOCK)

    def extended(halo, own_ref, c):
        return jnp.concatenate([halo[0, c], own_ref[c], halo[1, c]], axis=0)

    u = [jnp.where(inside, extended(halo_u, disp, c), 0.0) for c in range(2)]
    force = [extended(halo_f, body, c) for c in range(2)]
    index = [jnp.where(inside, extended(halo_a, assign, p), 127) for p in range(4)]
    u_parts = strain_parts_ext(u)

    drained(c1.at[pl.ds(0, SLABS - 1)], recv.at[4])
    c2src[...] = jnp.sum(c1[...], axis=0)
    c2[r] = c2src[...]
    for device in far:
        push(c2src, c2.at[r], 12, recv.at[5], device)
    drained(c2.at[pl.ds(0, GROUPS - 1)], recv.at[5])
    square = jnp.concatenate([c2[...].reshape(GROUPS, 128), jnp.zeros((128 - GROUPS, 128), F32)], axis=0)
    by_label = square.T[0:16, :]
    hom_out[...] = by_label[0:12, 0:GROUPS]
    rows = [by_label[k : k + 1, :] for k in range(15)]
    offset = [rows[c] - sum(rows[3 + 3 * j + c] * rows[12 + j] for j in range(3)) for c in range(3)]
    size = sum(jnp.abs(rows[k]) for k in range(3, 12))
    scale = RANGE * jnp.max(size, axis=1, keepdims=True)
    inverse_scale = 1.0 / scale

    def looked(row, p):
        return jnp.take_along_axis(jnp.broadcast_to(row, (EXT, 128)), index[p], axis=1, mode="promise_in_bounds")

    def point_strain(shapes, p):
        d1x, d2y, d1y, d2x = shapes
        sp, tp = p % 2, p // 2
        return d1x[tp], d2y[sp], d1y[sp] + d2x[tp]

    stress = []
    for p in range(4):
        strain = point_strain(u_parts, p)
        cs = [looked(rows[3 + k], p) for k in range(9)]
        for k in range(9):
            tangent[p, k] = cs[k]
        stress.append(
            [
                looked(offset[c], p) + cs[c] * strain[0] + cs[3 + c] * strain[1] + cs[6 + c] * strain[2]
                for c in range(3)
            ]
        )
    forces = assemble(stress)
    vector = [jnp.where(inside, force[c] - forces[c], 0.0) for c in range(2)]
    history = [vector]
    basis[0, 0], basis[0, 1] = vector[0][8:40], vector[1][8:40]

    def stiffness(field):
        shapes = strain_parts_ext(field)
        result = []
        for p in range(4):
            strain = point_strain(shapes, p)
            result.append(
                [
                    tangent[p, c] * strain[0] + tangent[p, 3 + c] * strain[1] + tangent[p, 6 + c] * strain[2]
                    for c in range(3)
                ]
            )
        return assemble(result)

    for k in range(CG_STEPS):
        image = stiffness(history[k])
        shifted = [jnp.where(inside, image[c] * inverse_scale - history[k][c], 0.0) for c in range(2)]
        if k:
            shifted = [2.0 * shifted[c] - history[k - 1][c] for c in range(2)]
        history.append(shifted)
        basis[k + 1, 0], basis[k + 1, 1] = shifted[0][8:40], shifted[1][8:40]

    dots = []
    for i, j in PAIRS:
        product = basis[i, 0] * basis[j, 0] + basis[i, 1] * basis[j, 1]
        dots.append(jnp.sum(product.reshape(4, 8, 128), axis=(0, 1), keepdims=True).reshape(1, 128))
    dots += [jnp.zeros((1, 128), F32)] * (16 - len(dots))
    stacked = jnp.sum(jnp.concatenate(dots, axis=0), axis=1, keepdims=True)
    diagonal = lax.broadcasted_iota(jnp.int32, (16, 128), 0) == lane_iota((16, 128))
    d1src[...] = jnp.sum(jnp.where(diagonal, stacked, 0.0), axis=0, keepdims=True)
    d1[s] = d1src[...]
    for device in peers:
        push(d1src, d1.at[s], 13, recv.at[6], device)
    drained(d1.at[pl.ds(0, SLABS - 1)], recv.at[6])
    d2src[...] = jnp.sum(d1[...], axis=0)
    d2[r] = d2src[...]
    for device in far:
        push(d2src, d2.at[r], 14, recv.at[7], device)
    drained(d2.at[pl.ds(0, GROUPS - 1)], recv.at[7])
    gram_row = jnp.sum(d2[...], axis=0)
    gram = {}
    for k, (i, j) in enumerate(PAIRS):
        value = jnp.sum(jnp.where(lane1 == k, gram_row, 0.0), axis=1, keepdims=True)
        gram[i, j] = gram[j, i] = value

    def inner(one, two):
        return sum(one[i] * two[j] * gram[i, j] for i in range(len(one)) for j in range(len(two)))

    def apply(coefficients):
        n = len(coefficients)
        result = [scale * c for c in coefficients] + [0.0]
        for k in range(n):
            if k == 0:
                result[1] = result[1] + scale * coefficients[0]
            else:
                result[k + 1] = result[k + 1] + 0.5 * scale * coefficients[k]
                result[k - 1] = result[k - 1] + 0.5 * scale * coefficients[k]
        return result

    one = jnp.ones((1, 1), F32)
    direction, residual = [one], [one]
    answer = []
    rho = gram[0, 0]
    for step in range(CG_STEPS):
        image = apply(direction)
        alpha = rho / inner(direction, image)
        answer = [
            (answer[k] if k < len(answer) else 0.0) + alpha * direction[k] for k in range(len(direction))
        ]
        if step == CG_STEPS - 1:
            break
        residual = [
            (residual[k] if k < len(residual) else 0.0) - alpha * image[k] for k in range(len(image))
        ]
        fresh = inner(residual, residual)
        beta = fresh / rho
        direction = [
            residual[k] + (beta * direction[k] if k < len(direction) else 0.0) for k in range(len(residual))
        ]
        rho = fresh
    for c in range(2):
        correction_out[c] = sum(answer[k] * basis[k, c] for k in range(CG_STEPS))

    drained(a1.at[pl.ds(0, SLABS - 1)], send.at[0])

    @pl.when(s == 0)
    def _():
        drained(a1, send.at[1])

    drained(pf.at[0, pl.ds(0, 3)], send.at[2])
    drained(pf.at[0], send.at[3])
    for k, halo in enumerate((halo_u, halo_f, halo_a)):
        drained(halo.at[1], send.at[4 + 2 * k])
        drained(halo.at[0], send.at[5 + 2 * k])
    drained(a2.at[pl.ds(0, GROUPS - 1)], send.at[10])
    drained(c1.at[pl.ds(0, SLABS - 1)], send.at[11])
    drained(c2.at[pl.ds(0, GROUPS - 1)], send.at[12])
    drained(d1.at[pl.ds(0, SLABS - 1)], send.at[13])
    drained(d2.at[pl.ds(0, GROUPS - 1)], send.at[14])


def write_kernel(one, two_a, two_b, two_c, three, one_out, two_out, three_out, sems):
    copies = [
        pltpu.make_async_copy(source, target, sems.at[k])
        for k, (source, target) in enumerate(
            (
                (one, one_out),
                (two_a, two_out.at[0, 0]),
                (two_b, two_out.at[0, 1]),
                (two_c, two_out.at[0, 2]),
                (three, three_out),
            )
        )
    ]
    for copy in copies:
        copy.start()
    for copy in copies:
        copy.wait()


def written(*values):
    return pl.pallas_call(
        write_kernel,
        out_shape=(
            jax.ShapeDtypeStruct((2, BLOCK, 128), F32),
            jax.ShapeDtypeStruct((1, 3, BLOCK, GRID), F32),
            jax.ShapeDtypeStruct((12, GROUPS), F32),
        ),
        in_specs=[pl.BlockSpec(memory_space=pl.ANY)] * 5,
        out_specs=(pl.BlockSpec(memory_space=pltpu.HBM),) * 3,
        scratch_shapes=[pltpu.SemaphoreType.DMA((5,))],
        compiler_params=pltpu.CompilerParams(vmem_limit_bytes=4 * 1024 * 1024),
        name="write_out",
    )(*values)


def shards(displacement, body_force, assignment, phases, flags):
    vmem = pl.BlockSpec(memory_space=pltpu.VMEM)
    row = lambda n: pltpu.VMEM((n, 1, 128), F32)
    one_row = pltpu.VMEM((1, 128), F32)
    square = (GRID, GRID)
    results = pl.pallas_call(
        kernel,
        out_shape=(
            jax.ShapeDtypeStruct((2, BLOCK, 128), F32),
            jax.ShapeDtypeStruct((BLOCK, GRID), F32),
            jax.ShapeDtypeStruct((BLOCK, GRID), F32),
            jax.ShapeDtypeStruct((BLOCK, GRID), F32),
            jax.ShapeDtypeStruct((12, GROUPS), F32),
        ),
        in_specs=[pl.BlockSpec(memory_space=pltpu.HBM)] * 5,
        out_specs=(vmem,) * 5,
        scratch_shapes=[
            pltpu.VMEM((2, BLOCK, 128), F32),
            pltpu.VMEM((2, BLOCK, 128), F32),
            pltpu.VMEM((4, BLOCK, 128), jnp.int32),
            pltpu.VMEM((4,) + square, BF16),
            pltpu.VMEM((2, 4, 2, BLOCK, GRID), jnp.int32),
            pltpu.VMEM((8, 128), F32),
            pltpu.VMEM((SLABS, 8, 128), F32),
            pltpu.VMEM((8, 128), F32),
            one_row, row(GROUPS), one_row, row(SLABS), one_row, row(GROUPS),
            one_row, row(SLABS), one_row, row(GROUPS),
            pltpu.VMEM((2, 2, 8, 128), F32),
            pltpu.VMEM((2, 2, 8, 128), F32),
            pltpu.VMEM((2, 4, 8, 128), jnp.int32),
            pltpu.VMEM((8, BLOCK, 128), F32),
            pltpu.VMEM((4, BLOCK, 128), F32),
            pltpu.VMEM((4, GROUPS, 8, 128), F32),
            pltpu.VMEM((3,) + square, F32),
            pltpu.VMEM(square, F32),
            pltpu.VMEM(square, F32),
            pltpu.VMEM((6,) + square, BF16),
            pltpu.VMEM((6,) + square, BF16),
            pltpu.VMEM((6,) + square, F32),
            pltpu.VMEM((6,) + square, BF16),
            pltpu.VMEM((6,) + square, BF16),
            pltpu.VMEM((6,) + square, F32),
            pltpu.VMEM((6, HALF, GRID), F32),
            pltpu.VMEM((CG_STEPS + 1, 2, BLOCK, 128), F32),
            pltpu.VMEM((4, 9, EXT, 128), F32),
            pltpu.SemaphoreType.DMA((5,)),
            pltpu.SemaphoreType.DMA((15,)),
            pltpu.SemaphoreType.DMA((8,)),
            pltpu.SemaphoreType.DMA((4,)),
            pltpu.SemaphoreType.DMA((3, 2)),
        ],
        compiler_params=pltpu.CompilerParams(
            collective_id=0, has_side_effects=True, vmem_limit_bytes=55080 * 1024
        ),
        name="fe2_step",
    )(displacement, body_force, assignment, phases, flags)
    return written(*results)


def solution(mesh):
    return jax.shard_map(
        shards,
        mesh=mesh,
        in_specs=(
            P(None, ("rve", "slab"), None),
            P(None, ("rve", "slab"), None),
            P(None, ("rve", "slab"), None),
            P("rve", "slab", None),
            P("rve", "slab", None),
        ),
        out_specs=(P(None, ("rve", "slab"), None), P("rve", None, "slab", None), P()),
        check_vma=False,
    )
```

```python
import math

import jax
import jax.numpy as jnp
from jax import lax
from jax.experimental import pallas as pl
from jax.experimental.pallas import tpu as pltpu
from jax.sharding import PartitionSpec as P

MESH = pl.DeviceIdType.MESH
F32 = jnp.float32
BF16 = jnp.bfloat16

GRID = 256
HALF = 128
GROUPS = 32
SLABS = 8
BLOCK = 32
EXT = 48
CG_STEPS = 4

MU_REF = 2.0
LAMBDA_REF = 2.0
COUPLE = (LAMBDA_REF + MU_REF) / (MU_REF * (LAMBDA_REF + 2.0 * MU_REF))
LOWER = 0.5 - 0.5 / math.sqrt(3.0)
UPPER = 0.5 + 0.5 / math.sqrt(3.0)
ENDS = (LOWER, UPPER)
WEIGHT = 0.25
RANGE = 0.5

PAIRS = [(i, j) for i in range(CG_STEPS) for j in range(i, CG_STEPS + 1)]


def wave(slot, place):
    k = jnp.where(slot == HALF, HALF, lax.rem(slot, HALF))
    sine = slot > HALF
    turn = lax.bitwise_and(k * place + jnp.where(sine, 3 * GRID // 4, 0), GRID - 1)
    angle = (jnp.abs(turn - HALF) - GRID // 4).astype(F32) * (2.0 * math.pi / GRID)
    square = angle * angle
    value = 1.0 / 362880.0 - square * (1.0 / 39916800.0)
    for term in (1.0 / 5040.0, 1.0 / 120.0, 1.0 / 6.0, 1.0):
        value = term - square * value
    flat = (k == 0) | (k == HALF)
    return angle * value * jnp.where(flat, 1.0 / math.sqrt(GRID), math.sqrt(2.0 / GRID))


OFFSETS = sorted(
    ((dx, dz) for dx in range(4) for dz in range(8) if dx or dz),
    key=lambda o: -(min(o[0], 4 - o[0]) + min(o[1], 8 - o[1])),
)
NEAR = sorted(
    ((dy, dc) for dy in range(4) for dc in range(2) if dy or dc),
    key=lambda o: (-min(o[0], 4 - o[0]), -o[1]),
)


def lane_iota(shape):
    return lax.broadcasted_iota(jnp.int32, shape, len(shape) - 1)


def rows_up(field):
    rolled = pltpu.roll(field, field.shape[1] - 1, 1)
    return jnp.where(lane_iota(field.shape) == field.shape[1] - 1, 0.0, rolled)


def rows_down(field):
    rolled = pltpu.roll(field, 1, 1)
    return jnp.where(lane_iota(field.shape) == 0, 0.0, rolled)


def columns_back(field):
    return pltpu.roll(field, field.shape[0] - 1, 0)


def columns_on(field):
    return pltpu.roll(field, 1, 0)


def split(value):
    high = value.astype(BF16)
    return high, (value - high.astype(F32)).astype(BF16)


def dot(left, right):
    return jnp.dot(left, right, preferred_element_type=F32)


def strain_parts(first, second, first_next, second_next):
    slopes = []
    for here, beside in ((first, first_next), (second, second_next)):
        above = rows_up(here)
        both = rows_up(beside)
        across, across_up = beside - here, both - above
        up, up_next = above - here, both - beside
        slopes.append(
            (
                [(1.0 - t) * across + t * across_up for t in ENDS],
                [(1.0 - s) * up + s * up_next for s in ENDS],
            )
        )
    return slopes[0][0], slopes[1][1], slopes[0][1], slopes[1][0]


def strain_parts_ext(field):
    slopes = []
    for here in field:
        above = rows_up(here)
        beside, both = columns_back(here), columns_back(above)
        across, across_up = beside - here, both - above
        up, up_next = above - here, both - beside
        slopes.append(
            (
                [(1.0 - t) * across + t * across_up for t in ENDS],
                [(1.0 - s) * up + s * up_next for s in ENDS],
            )
        )
    return slopes[0][0], slopes[1][1], slopes[0][1], slopes[1][0]


def assemble(stress):
    by_t = lambda c, t: stress[2 * t][c] + stress[2 * t + 1][c]
    by_s = lambda c, s: stress[s][c] + stress[2 + s][c]

    def mixed(parts):
        low = sum(WEIGHT * (1.0 - ENDS[k]) * parts[k] for k in range(2))
        high = sum(WEIGHT * ENDS[k] * parts[k] for k in range(2))
        return low, high

    forces = []
    for normal_x, normal_y in ((0, 2), (2, 1)):
        low_x, high_x = mixed([by_t(normal_x, t) for t in range(2)])
        low_y, high_y = mixed([by_s(normal_y, s) for s in range(2)])
        on = low_x - high_y + rows_down(high_x + high_y)
        forces.append(columns_on(on) - (low_x + low_y) + rows_down(low_y - high_x))
    return forces


def inverse(value):
    guess = pl.reciprocal(value, approx=True)
    return guess * (2.0 - value * guess)


def law(strain, harden):
    volume = strain[0] + strain[1]
    normal = 0.5 * (strain[0] - strain[1])
    shear = 0.5 * strain[2]
    stiff = harden * (2.0 * normal * normal + 2.0 * shear * shear)
    factor = (1.0 + 2.0 * stiff) * inverse(1.0 + 3.0 * stiff)
    for turn in range(2):
        square = stiff * factor * factor
        factor = (1.0 + 2.0 * square * factor) * inverse(1.0 + 3.0 * square)
    square = factor * factor
    slope = -harden * square * factor * inverse(1.0 + 3.0 * stiff * square)
    return volume, normal, shear, factor, slope


def stress_of(state, bulk, modulus):
    volume, normal, shear, factor, slope = state
    spread = 2.0 * modulus * factor
    return [bulk * volume + spread * normal, bulk * volume - spread * normal, spread * shear]


def image_of(state, bulk, modulus, rest):
    volume, normal, shear, factor, slope = state
    d_volume = rest[0] + rest[1]
    d_normal = 0.5 * (rest[0] - rest[1])
    d_shear = 0.5 * rest[2]
    d_factor = slope * (4.0 * normal * d_normal + 4.0 * shear * d_shear)
    d_dev = 2.0 * modulus * (factor * d_normal + d_factor * normal)
    return [
        bulk * d_volume + d_dev,
        bulk * d_volume - d_dev,
        2.0 * modulus * (factor * d_shear + d_factor * shear),
    ]


def green(first, second, mixed, part_11, part_22, cross):
    across = cross * mixed
    one, two = part_11 * first + across, part_22 * second + across
    total = (2.0 * MU_REF * COUPLE / 2.0) * (one + two)
    return (
        one - part_11 * total,
        two - part_22 * total,
        cross * (first + second - 2.0 * total) + (part_11 + part_22) * mixed,
    )


def kernel(
    disp_hbm, body_hbm, assign_hbm, phase_hbm, flag_hbm,
    correction_out, strain_0, strain_1, strain_2, hom_out,
    disp, body, assign, table, pf, a1src, a1, nb, a2src, a2, c1src, c1, c2src, c2, d1src, d1, d2src, d2,
    halo_u, halo_f, halo_a,
    parts, labels, accs, green_tab, ph_f, hard_f, mid_h, mid_l, spec, filt_h, filt_l,
    strains, last, basis, tangent,
    relay, load, send, recv, gather_recv, halo_recv,
):
    r = lax.axis_index("rve")
    s = lax.axis_index("slab")
    y, core = s // 2, s % 2
    half, lane_field = s // 4, s % 4
    before, after = lax.rem(r + GROUPS - 1, GROUPS), lax.rem(r + 1, GROUPS)
    peers = [(r, lax.rem(y + dy, 4) * 2 + (1 - core if dc else core)) for dy, dc in NEAR]
    gx, gz = r // 8, r % 8
    far = [(lax.rem(gx + dx, 4) * 8 + lax.rem(gz + dz, 8), s) for dx, dz in OFFSETS]
    left = (jnp.where(s == 0, before, r), lax.rem(s + SLABS - 1, SLABS))
    right = (jnp.where(s == SLABS - 1, after, r), lax.rem(s + 1, SLABS))

    loads = [
        pltpu.make_async_copy(source, target, load.at[k])
        for k, (source, target) in enumerate(
            (
                (disp_hbm, disp),
                (assign_hbm, assign),
                (phase_hbm.at[0], pf.at[core, y, 0]),
                (flag_hbm.at[0], pf.at[core, y, 1]),
                (body_hbm, body),
            )
        )
    ]
    for copy in loads:
        copy.start()

    barrier = pltpu.get_barrier_semaphore()

    def greet(device):
        pl.semaphore_signal(barrier, inc=1, device_id=device, device_id_type=MESH)

    ring_z = {dz: (gx * 8 + lax.rem(gz + dz, 8), s) for dz in (1, 2, 6, 7)}
    ring_x = [(lax.rem(gx + dx, 4) * 8 + gz, s) for dx in (2, 1, 3)]
    opposite = y == 2
    across = (jnp.where(opposite, before, after), jnp.where(opposite, SLABS - 1, 0))
    has_across = jnp.where(opposite, r > 0, r < GROUPS - 1)
    gives_back, gives_on = (s == 0) & (r > 0), (s == SLABS - 1) & (r < GROUPS - 1)
    has_left, has_right = (s > 0) | (r > 0), (s < SLABS - 1) | (r < GROUPS - 1)

    @pl.when(has_across)
    def _():
        greet(across)

    @pl.when(gives_back)
    def _():
        for k in (0, 1, 2, 3, 6, 7):
            greet((before, k))

    @pl.when(gives_on)
    def _():
        for k in (4, 5):
            greet((after, k))

    for device in [ring_z[2], ring_z[6]] + ring_x + peers + [ring_z[1], ring_z[7]]:
        greet(device)

    def label_sums(rows, count):
        step = rows // 8

        def one(label, _):
            e = [parts[k, 0:rows, :] for k in range(8)]
            mask = [jnp.where(labels[p, 0:rows, :] == label.astype(F32), 1.0, 0.0) for p in range(4)]
            t_low, t_high = mask[0] + mask[1], mask[2] + mask[3]
            s_low, s_high = mask[0] + mask[2], mask[1] + mask[3]
            sums = [
                e[0] * t_low + e[1] * t_high,
                e[2] * s_low + e[3] * s_high,
                e[4] * s_low + e[5] * s_high + e[6] * t_low + e[7] * t_high,
            ]
            if count:
                sums.append(t_low + t_high)
            for c in range(len(sums)):
                accs[c, label] = jnp.sum(sums[c].reshape(step, 8, 128), axis=0)
            return 0

        lax.fori_loop(0, GROUPS, one, 0, unroll=GROUPS if rows == 8 else 4)
        used = 4 if count else 3
        folded = jnp.sum(accs[0:used].reshape(used * GROUPS, 8, 128), axis=1)
        if not count:
            folded = jnp.concatenate([folded, jnp.zeros((GROUPS, 128), F32)], axis=0)
        ones = jnp.ones((8, 128), BF16)
        total = jnp.zeros((8, 128), F32)
        for turn in range(3):
            piece = folded.astype(BF16)
            folded = folded - piece.astype(F32)
            total = total + lax.dot_general(
                ones, piece, (((1,), (1,)), ((), ())), preferred_element_type=F32
            )
        return total[0:1, :]

    def keep_parts(fields, rows):
        d1x, d2y, d1y, d2x = strain_parts(*fields)
        for k, value in enumerate(d1x + d2y + d1y + d2x):
            parts[k, 0:rows, :] = value

    row_of = lax.broadcasted_iota(jnp.int32, (BLOCK, 128), 0)
    loads[0].wait()
    loads[1].wait()
    own = [disp[0], disp[1]]
    beside = [jnp.where(row_of == BLOCK - 1, 0.0, columns_back(u)) for u in own]
    keep_parts(own + beside, BLOCK)
    for p in range(4):
        labels[p] = assign[p].astype(F32)
    a1src[...] = jnp.concatenate(
        [label_sums(BLOCK, True), disp[0, 0:1, :], disp[1, 0:1, :]]
        + [labels[p, BLOCK - 1 : BLOCK, :] for p in range(4)]
        + [jnp.zeros((1, 128), F32)],
        axis=0,
    )
    a1[s] = a1src[...]

    for copy in loads[2:5]:
        copy.wait()
    pl.semaphore_wait(
        barrier,
        SLABS - 1 + 3 + 4 + jnp.where(has_across, 1, 0) + jnp.where(gives_back, 6, 0) + jnp.where(gives_on, 2, 0),
    )

    def push(source, target, k, recv_sem, device):
        pltpu.make_async_remote_copy(
            source, target, send.at[k], recv_sem, device_id=device, device_id_type=MESH
        ).start()

    def drained(ref, sem):
        pltpu.make_async_copy(ref, ref, sem).wait()

    @pl.when(gives_back)
    def _():
        for k in (0, 1, 2, 3, 6, 7):
            push(a1src, nb, 1, recv.at[1], (before, k))

    @pl.when(gives_on)
    def _():
        for k in (4, 5):
            push(a1src, nb, 1, recv.at[1], (after, k))

    for device in peers:
        push(a1src, a1.at[s], 0, recv.at[0], device)

    sibling = (r, y * 2 + 1 - core)
    for k in range(1, 4):
        push(pf.at[core, y], pf.at[core, y], 2, gather_recv.at[y], (r, lax.rem(y + k, 4) * 2 + core))
    push(pf.at[core, y], pf.at[core, y], 3, recv.at[2], sibling)

    strip = ((disp, halo_u), (body, halo_f), (assign, halo_a))

    @pl.when(has_left)
    def _():
        for k, (own_ref, halo) in enumerate(strip):
            push(own_ref.at[:, pl.ds(0, 8), :], halo.at[1], 4 + 2 * k, halo_recv.at[k, 1], left)

    @pl.when(has_right)
    def _():
        for k, (own_ref, halo) in enumerate(strip):
            push(own_ref.at[:, pl.ds(BLOCK - 8, 8), :], halo.at[0], 5 + 2 * k, halo_recv.at[k, 0], right)

    def tell(k, devices):
        for device in devices:
            pl.semaphore_signal(relay.at[k], inc=1, device_id=device, device_id_type=MESH)

    tell(0, [ring_z[2], ring_z[6]])
    def symbols(k, _):
        rows = pl.ds(pl.multiple_of(k * 32, 32), 32)
        row = lax.broadcasted_iota(jnp.int32, (32, GRID), 0) + k * 32
        lane = lax.broadcasted_iota(jnp.int32, (32, GRID), 1)
        k1 = lax.rem(row, HALF).astype(F32)
        k2 = lax.rem(lane, HALF).astype(F32)
        square = k1 * k1 + k2 * k2
        inverse = jnp.where(square > 0.0, 1.0 / jnp.maximum(square, 1.0), 0.0)
        sign = jnp.where((row < HALF) == (lane < HALF), -1.0, 1.0)
        green_tab[0, rows, :] = k1 * k1 * inverse
        green_tab[1, rows, :] = k2 * k2 * inverse
        green_tab[2, rows, :] = sign * k1 * k2 * inverse
        table[0, rows, :], table[1, rows, :] = split(wave(row, lane))
        table[2, rows, :], table[3, rows, :] = split(wave(lane, row))
        return 0

    lax.fori_loop(0, 8, symbols, 0)

    pl.semaphore_wait(relay.at[0], 2)
    tell(1, ring_x)

    drained(a1.at[pl.ds(0, SLABS - 1)], recv.at[0])
    @pl.when(has_across)
    def _():
        drained(nb, recv.at[1])

    @pl.when(jnp.logical_not(has_across))
    def _():
        nb[...] = jnp.zeros((8, 128), F32)

    row8 = lax.broadcasted_iota(jnp.int32, (8, 128), 0)
    gathered = a1[...]
    counted = jnp.where(has_across, 1.0, 0.0)
    nxt = []
    for c in range(2):
        own_c = jnp.concatenate([gathered[k, 1 + c : 2 + c, :] for k in range(SLABS)], axis=0)
        outer = jnp.where(opposite, gathered[0, 1 + c : 2 + c, :], nb[1 + c : 2 + c, :]) * counted
        nxt.append(jnp.where(row8 == 7, outer, columns_back(own_c)))
    zero8 = jnp.zeros((8, 128), F32)
    keep_parts([zero8, zero8] + nxt, 8)
    for p in range(4):
        outer = jnp.where(opposite, nb[3 + p : 4 + p, :], gathered[SLABS - 1, 3 + p : 4 + p, :])
        labels[p, 0:8, :] = jnp.concatenate(
            [gathered[k, 3 + p : 4 + p, :] for k in range(SLABS - 1)] + [outer], axis=0
        )
    a2src[...] = label_sums(8, False) + jnp.sum(gathered, axis=0)[0:1, :]
    a2[r] = a2src[...]
    pl.semaphore_wait(relay.at[1], 3)
    for device in far:
        push(a2src, a2.at[r], 10, recv.at[3], device)

    def take_block(slab, chip):
        rows = pl.ds(pl.multiple_of((chip * 2 + slab) * BLOCK, BLOCK), BLOCK)
        here = pf[slab, chip, 0].astype(F32)
        active = pf[slab, chip, 1].astype(F32)
        ph_f[rows, :] = here
        hard_f[rows, :] = active * (2.0 - 1.5 * here)
        kinds_of = [here.astype(BF16), active.astype(BF16), (here * active).astype(BF16)]
        block = jnp.concatenate(kinds_of, axis=0)
        value = dot(block, table[2]) + dot(block, table[3])
        for m in range(3):
            part_h, part_l = split(value[m * BLOCK : (m + 1) * BLOCK])
            mid_h[m, rows, :] = part_h
            mid_l[m, rows, :] = part_l

    take_block(core, y)
    for k in range(1, 4):
        other = lax.rem(y + k, 4)
        drained(pf.at[core, other], gather_recv.at[other])
        push(pf.at[core, other], pf.at[core, other], 3, recv.at[2], sibling)
        take_block(core, other)
    drained(pf.at[1 - core], recv.at[2])
    for k in range(4):
        take_block(1 - core, k)

    def along_x(high, low, rows=slice(None), which=0):
        left_h, left_l = table[which, rows, :], table[which + 1, rows, :]
        return dot(left_h, high) + dot(left_h, low) + dot(left_l, high)

    def along_y(high, low, which):
        right_h, right_l = table[which], table[which + 1]
        return dot(high, right_h) + dot(high, right_l) + dot(low, right_h)

    for m in range(3):
        spec[m] = along_x(mid_h[m], mid_l[m])

    drained(a2.at[pl.ds(0, GROUPS - 1)], recv.at[3])
    totals = jnp.sum(a2[...], axis=0)
    lane1 = lane_iota((1, 128))
    picked = [
        jnp.sum(jnp.where(lane1 == 32 * c + r, totals, 0.0), axis=1, keepdims=True) for c in range(4)
    ]
    mean = [jnp.broadcast_to(picked[c] / picked[3], (8, 128)) for c in range(3)]
    unit = [jnp.where(lane_field == c, 1.0, 0.0) + jnp.where((lane_field == 3) & (c == 2), 1.0, 0.0) for c in range(3)]
    units = [jnp.full((8, 128), u, F32) for u in unit]

    kinds = {}
    for p in range(2):
        bulk, modulus = (6.0, 3.0) if p else (2.0, 1.0)
        for f in range(2):
            state = law(mean, (0.5 if p else 2.0) * f)
            kinds[p, f] = stress_of(state, bulk / MU_REF, modulus / MU_REF) + image_of(
                state, bulk / MU_REF, modulus / MU_REF, units
            )
    weights = []
    for k in range(6):
        base = kinds[0, 0][k]
        by_phase = kinds[1, 0][k] - base
        by_flag = kinds[0, 1][k] - base
        weights.append((by_phase, by_flag, kinds[1, 1][k] - base - by_phase - by_flag))

    def filter_pieces(load, n):
        def piece(k):
            for a in range(2):
                rows = slice(a * HALF + k * 16, a * HALF + k * 16 + 16)
                swap_rows = slice((1 - a) * HALF + k * 16, (1 - a) * HALF + k * 16 + 16)
                for b in range(2):
                    lanes = slice(b * HALF, (b + 1) * HALF)
                    swap_lanes = slice((1 - b) * HALF, (2 - b) * HALF)
                    sym = [green_tab[i, rows, lanes] for i in range(3)]
                    out = green(*load(n, rows, lanes, swap_rows, swap_lanes), *sym)
                    for c in range(3):
                        rr, ll = (swap_rows, swap_lanes) if c == 2 else (rows, lanes)
                        high, low = split(out[c])
                        filt_h[3 * n + c, rr, ll] = high
                        filt_l[3 * n + c, rr, ll] = low

        return [lambda k=k: piece(k) for k in range(8)]

    def together(first, second):
        turns = max(len(first), len(second))
        for k in range(turns):
            for pieces in (first, second):
                for j in range(k * len(pieces) // turns, (k + 1) * len(pieces) // turns):
                    pieces[j]()

    def wide(value):
        return jnp.concatenate([value, value], axis=0)

    wide_weights = [[wide(w) for w in three] for three in weights]

    def load_first(n, rows, lanes, swap_rows, swap_lanes):
        here = [spec[m, rows, lanes] for m in range(3)]
        there = [spec[m, swap_rows, swap_lanes] for m in range(3)]
        mix = lambda k, fields: sum(wide_weights[k][m] * fields[m] for m in range(3))
        return mix(3 * n, here), mix(3 * n + 1, here), mix(3 * n + 2, there)

    start = mean + units

    def invert_first(n):
        def one(k):
            high, low = split(along_x(filt_h[k], filt_l[k], which=2))
            strains[k] = jnp.broadcast_to(start[k][0:1, 0:1], (GRID, GRID)) - along_y(high, low, 0)

        return [lambda k=k: one(k) for k in range(3 * n, 3 * n + 3)]

    for piece in filter_pieces(load_first, 0):
        piece()
    together(filter_pieces(load_first, 1), invert_first(0))
    for piece in invert_first(1):
        piece()

    def material(k):
        rows = slice(k * 16, k * 16 + 16)
        for b in range(2):
            lanes = slice(b * HALF, (b + 1) * HALF)
            here = ph_f[rows, lanes]
            state = law([strains[c, rows, lanes] for c in range(3)], hard_f[rows, lanes])
            bulk, modulus = 1.0 + 2.0 * here, 0.5 + here
            values = stress_of(state, bulk, modulus) + image_of(
                state, bulk, modulus, [strains[3 + c, rows, lanes] for c in range(3)]
            )
            for c in range(6):
                filt_h[c, rows, lanes], filt_l[c, rows, lanes] = split(values[c])

    def forward_y(q):
        rows = slice(q * 64, q * 64 + 64)
        stacked = lambda ref: jnp.concatenate([ref[c, rows, :] for c in range(6)], axis=0)
        high, low = split(along_y(stacked(filt_h), stacked(filt_l), 2))
        for c in range(6):
            mid_h[c, rows, :] = high[c * 64 : c * 64 + 64]
            mid_l[c, rows, :] = low[c * 64 : c * 64 + 64]

    for q in range(5):
        pieces = [lambda k=k: material(k) for k in range(4 * q, 4 * q + 4)] if q < 4 else []
        together(pieces, [lambda: forward_y(q - 1)] if q else [])

    def load_second(n, rows, lanes, swap_rows, swap_lanes):
        return spec[3 * n, rows, lanes], spec[3 * n + 1, rows, lanes], spec[3 * n + 2, swap_rows, swap_lanes]

    part = pl.ds(pl.multiple_of(half * HALF, HALF), HALF)

    def forward_x(n):
        def one(k):
            spec[k] = along_x(mid_h[k], mid_l[k])

        return [lambda k=k: one(k) for k in range(3 * n, 3 * n + 3)]

    def invert_second(n):
        def one(k):
            high, low = split(along_x(filt_h[k], filt_l[k], rows=part, which=2))
            last[k] = strains[k, part, :] - along_y(high, low, 0)

        return [lambda k=k: one(k) for k in range(3 * n, 3 * n + 3)]

    for piece in forward_x(0):
        piece()
    together(filter_pieces(load_second, 0), forward_x(1))
    together(filter_pieces(load_second, 1), invert_second(0))
    for piece in invert_second(1):
        piece()

    def finish(k, sums):
        rows = pl.ds(pl.multiple_of(k * 16, 16), 16)
        full = pl.ds(pl.multiple_of(half * HALF + k * 16, 16), 16)
        sums = list(sums)
        for b in range(2):
            lanes = slice(b * HALF, (b + 1) * HALF)
            here = ph_f[full, lanes]
            state = law([last[c, rows, lanes] for c in range(3)], hard_f[full, lanes])
            bulk, modulus = 2.0 + 4.0 * here, 1.0 + 2.0 * here
            values = stress_of(state, bulk, modulus) + image_of(
                state, bulk, modulus, [last[3 + c, rows, lanes] for c in range(3)]
            )
            for c in range(6):
                sums[c] = sums[c] + values[c][0:8, :] + values[c][8:16, :]
        return tuple(sums)

    sums = lax.fori_loop(0, 8, finish, tuple(jnp.zeros((8, 128), F32) for c in range(6)), unroll=4)
    for c, strain_out in enumerate((strain_0, strain_1, strain_2)):
        strain_out[...] = last[c, pl.ds(pl.multiple_of(lane_field * BLOCK, BLOCK), BLOCK), :]

    message = jnp.zeros((1, 128), F32)
    for c in range(3):
        stress_sum, image_sum = [
            jnp.sum(jnp.sum(sums[k], axis=0, keepdims=True), axis=1, keepdims=True) * (1.0 / (GRID * GRID))
            for k in (c, 3 + c)
        ]
        message = message + jnp.where((lane1 == c) & (lane_field == 0), stress_sum, 0.0)
        message = message + jnp.where((lane1 == 3 + 3 * lane_field + c) & (lane_field < 3), image_sum, 0.0)
        message = message + jnp.where((lane1 == 12 + c) & (s == 0), mean[c][0:1, :], 0.0)
    c1src[...] = message
    c1[s] = message
    for device in peers:
        push(c1src, c1.at[s], 11, recv.at[4], device)

    for side, has_side in enumerate((has_left, has_right)):

        @pl.when(has_side)
        def _():
            for k, (own_ref, halo) in enumerate(strip):
                drained(halo.at[side], halo_recv.at[k, side])

        @pl.when(jnp.logical_not(has_side))
        def _():
            for own_ref, halo in strip:
                halo[side] = jnp.zeros(halo.shape[1:], halo.dtype)

    column = lax.broadcasted_iota(jnp.int32, (EXT, 128), 0) + ((r * SLABS + s) * BLOCK - 8)
    inside = (column >= 0) & (column < GROUPS * SLABS * BLOCK)

    def extended(halo, own_ref, c):
        return jnp.concatenate([halo[0, c], own_ref[c], halo[1, c]], axis=0)

    u = [jnp.where(inside, extended(halo_u, disp, c), 0.0) for c in range(2)]
    force = [extended(halo_f, body, c) for c in range(2)]
    index = [jnp.where(inside, extended(halo_a, assign, p), 127) for p in range(4)]
    u_parts = strain_parts_ext(u)

    drained(c1.at[pl.ds(0, SLABS - 1)], recv.at[4])
    c2src[...] = jnp.sum(c1[...], axis=0)
    c2[r] = c2src[...]
    for device in far:
        push(c2src, c2.at[r], 12, recv.at[5], device)
    drained(c2.at[pl.ds(0, GROUPS - 1)], recv.at[5])
    square = jnp.concatenate([c2[...].reshape(GROUPS, 128), jnp.zeros((128 - GROUPS, 128), F32)], axis=0)
    by_label = square.T[0:16, :]
    hom_out[...] = by_label[0:12, 0:GROUPS]
    rows = [by_label[k : k + 1, :] for k in range(15)]
    offset = [rows[c] - sum(rows[3 + 3 * j + c] * rows[12 + j] for j in range(3)) for c in range(3)]
    size = sum(jnp.abs(rows[k]) for k in range(3, 12))
    scale = RANGE * jnp.max(size, axis=1, keepdims=True)
    inverse_scale = 1.0 / scale

    def looked(row, p):
        return jnp.take_along_axis(jnp.broadcast_to(row, (EXT, 128)), index[p], axis=1, mode="promise_in_bounds")

    def point_strain(shapes, p):
        d1x, d2y, d1y, d2x = shapes
        sp, tp = p % 2, p // 2
        return d1x[tp], d2y[sp], d1y[sp] + d2x[tp]

    stress = []
    for p in range(4):
        strain = point_strain(u_parts, p)
        cs = [looked(rows[3 + k], p) for k in range(9)]
        for k in range(9):
            tangent[p, k] = cs[k]
        stress.append(
            [
                looked(offset[c], p) + cs[c] * strain[0] + cs[3 + c] * strain[1] + cs[6 + c] * strain[2]
                for c in range(3)
            ]
        )
    forces = assemble(stress)
    vector = [jnp.where(inside, force[c] - forces[c], 0.0) for c in range(2)]
    history = [vector]
    basis[0, 0], basis[0, 1] = vector[0][8:40], vector[1][8:40]

    def stiffness(field):
        shapes = strain_parts_ext(field)
        result = []
        for p in range(4):
            strain = point_strain(shapes, p)
            result.append(
                [
                    tangent[p, c] * strain[0] + tangent[p, 3 + c] * strain[1] + tangent[p, 6 + c] * strain[2]
                    for c in range(3)
                ]
            )
        return assemble(result)

    for k in range(CG_STEPS):
        image = stiffness(history[k])
        shifted = [jnp.where(inside, image[c] * inverse_scale - history[k][c], 0.0) for c in range(2)]
        if k:
            shifted = [2.0 * shifted[c] - history[k - 1][c] for c in range(2)]
        history.append(shifted)
        basis[k + 1, 0], basis[k + 1, 1] = shifted[0][8:40], shifted[1][8:40]

    dots = []
    for i, j in PAIRS:
        product = basis[i, 0] * basis[j, 0] + basis[i, 1] * basis[j, 1]
        dots.append(jnp.sum(product.reshape(4, 8, 128), axis=(0, 1), keepdims=True).reshape(1, 128))
    dots += [jnp.zeros((1, 128), F32)] * (16 - len(dots))
    stacked = jnp.sum(jnp.concatenate(dots, axis=0), axis=1, keepdims=True)
    diagonal = lax.broadcasted_iota(jnp.int32, (16, 128), 0) == lane_iota((16, 128))
    d1src[...] = jnp.sum(jnp.where(diagonal, stacked, 0.0), axis=0, keepdims=True)
    d1[s] = d1src[...]
    for device in peers:
        push(d1src, d1.at[s], 13, recv.at[6], device)
    drained(d1.at[pl.ds(0, SLABS - 1)], recv.at[6])
    d2src[...] = jnp.sum(d1[...], axis=0)
    d2[r] = d2src[...]
    for device in far:
        push(d2src, d2.at[r], 14, recv.at[7], device)
    drained(d2.at[pl.ds(0, GROUPS - 1)], recv.at[7])
    gram_row = jnp.sum(d2[...], axis=0)
    gram = {}
    for k, (i, j) in enumerate(PAIRS):
        value = jnp.sum(jnp.where(lane1 == k, gram_row, 0.0), axis=1, keepdims=True)
        gram[i, j] = gram[j, i] = value

    def inner(one, two):
        return sum(one[i] * two[j] * gram[i, j] for i in range(len(one)) for j in range(len(two)))

    def apply(coefficients):
        n = len(coefficients)
        result = [scale * c for c in coefficients] + [0.0]
        for k in range(n):
            if k == 0:
                result[1] = result[1] + scale * coefficients[0]
            else:
                result[k + 1] = result[k + 1] + 0.5 * scale * coefficients[k]
                result[k - 1] = result[k - 1] + 0.5 * scale * coefficients[k]
        return result

    one = jnp.ones((1, 1), F32)
    direction, residual = [one], [one]
    answer = []
    rho = gram[0, 0]
    for step in range(CG_STEPS):
        image = apply(direction)
        alpha = rho / inner(direction, image)
        answer = [
            (answer[k] if k < len(answer) else 0.0) + alpha * direction[k] for k in range(len(direction))
        ]
        if step == CG_STEPS - 1:
            break
        residual = [
            (residual[k] if k < len(residual) else 0.0) - alpha * image[k] for k in range(len(image))
        ]
        fresh = inner(residual, residual)
        beta = fresh / rho
        direction = [
            residual[k] + (beta * direction[k] if k < len(direction) else 0.0) for k in range(len(residual))
        ]
        rho = fresh
    for c in range(2):
        correction_out[c] = sum(answer[k] * basis[k, c] for k in range(CG_STEPS))

    drained(a1.at[pl.ds(0, SLABS - 1)], send.at[0])

    @pl.when(gives_back)
    def _():
        drained(a1.at[pl.ds(0, 6)], send.at[1])

    @pl.when(gives_on)
    def _():
        drained(a1.at[pl.ds(0, 2)], send.at[1])

    drained(pf.at[0, pl.ds(0, 3)], send.at[2])
    drained(pf.at[0], send.at[3])
    for side, has_side in enumerate((has_left, has_right)):

        @pl.when(has_side)
        def _():
            for k, (own_ref, halo) in enumerate(strip):
                drained(halo.at[side], send.at[4 + 2 * k + side])

    drained(a2.at[pl.ds(0, GROUPS - 1)], send.at[10])
    drained(c1.at[pl.ds(0, SLABS - 1)], send.at[11])
    drained(c2.at[pl.ds(0, GROUPS - 1)], send.at[12])
    drained(d1.at[pl.ds(0, SLABS - 1)], send.at[13])
    drained(d2.at[pl.ds(0, GROUPS - 1)], send.at[14])


def write_kernel(one, two_a, two_b, two_c, three, one_out, two_out, three_out, sems):
    copies = [
        pltpu.make_async_copy(source, target, sems.at[k])
        for k, (source, target) in enumerate(
            (
                (one, one_out),
                (two_a, two_out.at[0, 0]),
                (two_b, two_out.at[0, 1]),
                (two_c, two_out.at[0, 2]),
                (three, three_out),
            )
        )
    ]
    for copy in copies:
        copy.start()
    for copy in copies:
        copy.wait()


def written(*values):
    return pl.pallas_call(
        write_kernel,
        out_shape=(
            jax.ShapeDtypeStruct((2, BLOCK, 128), F32),
            jax.ShapeDtypeStruct((1, 3, BLOCK, GRID), F32),
            jax.ShapeDtypeStruct((12, GROUPS), F32),
        ),
        in_specs=[pl.BlockSpec(memory_space=pl.ANY)] * 5,
        out_specs=(pl.BlockSpec(memory_space=pltpu.HBM),) * 3,
        scratch_shapes=[pltpu.SemaphoreType.DMA((5,))],
        compiler_params=pltpu.CompilerParams(vmem_limit_bytes=4 * 1024 * 1024),
        name="write_out",
    )(*values)


def shards(displacement, body_force, assignment, phases, flags):
    vmem = pl.BlockSpec(memory_space=pltpu.VMEM)
    row = lambda n: pltpu.VMEM((n, 1, 128), F32)
    one_row = pltpu.VMEM((1, 128), F32)
    square = (GRID, GRID)
    results = pl.pallas_call(
        kernel,
        out_shape=(
            jax.ShapeDtypeStruct((2, BLOCK, 128), F32),
            jax.ShapeDtypeStruct((BLOCK, GRID), F32),
            jax.ShapeDtypeStruct((BLOCK, GRID), F32),
            jax.ShapeDtypeStruct((BLOCK, GRID), F32),
            jax.ShapeDtypeStruct((12, GROUPS), F32),
        ),
        in_specs=[pl.BlockSpec(memory_space=pltpu.HBM)] * 5,
        out_specs=(vmem,) * 5,
        scratch_shapes=[
            pltpu.VMEM((2, BLOCK, 128), F32),
            pltpu.VMEM((2, BLOCK, 128), F32),
            pltpu.VMEM((4, BLOCK, 128), jnp.int32),
            pltpu.VMEM((4,) + square, BF16),
            pltpu.VMEM((2, 4, 2, BLOCK, GRID), jnp.int32),
            pltpu.VMEM((8, 128), F32),
            pltpu.VMEM((SLABS, 8, 128), F32),
            pltpu.VMEM((8, 128), F32),
            one_row, row(GROUPS), one_row, row(SLABS), one_row, row(GROUPS),
            one_row, row(SLABS), one_row, row(GROUPS),
            pltpu.VMEM((2, 2, 8, 128), F32),
            pltpu.VMEM((2, 2, 8, 128), F32),
            pltpu.VMEM((2, 4, 8, 128), jnp.int32),
            pltpu.VMEM((8, BLOCK, 128), F32),
            pltpu.VMEM((4, BLOCK, 128), F32),
            pltpu.VMEM((4, GROUPS, 8, 128), F32),
            pltpu.VMEM((3,) + square, F32),
            pltpu.VMEM(square, F32),
            pltpu.VMEM(square, F32),
            pltpu.VMEM((6,) + square, BF16),
            pltpu.VMEM((6,) + square, BF16),
            pltpu.VMEM((6,) + square, F32),
            pltpu.VMEM((6,) + square, BF16),
            pltpu.VMEM((6,) + square, BF16),
            pltpu.VMEM((6,) + square, F32),
            pltpu.VMEM((6, HALF, GRID), F32),
            pltpu.VMEM((CG_STEPS + 1, 2, BLOCK, 128), F32),
            pltpu.VMEM((4, 9, EXT, 128), F32),
            pltpu.SemaphoreType.REGULAR((2,)),
            pltpu.SemaphoreType.DMA((5,)),
            pltpu.SemaphoreType.DMA((15,)),
            pltpu.SemaphoreType.DMA((8,)),
            pltpu.SemaphoreType.DMA((4,)),
            pltpu.SemaphoreType.DMA((3, 2)),
        ],
        compiler_params=pltpu.CompilerParams(
            collective_id=0, has_side_effects=True, vmem_limit_bytes=55080 * 1024
        ),
        name="fe2_step",
    )(displacement, body_force, assignment, phases, flags)
    return written(*results)


def solution(mesh):
    return jax.shard_map(
        shards,
        mesh=mesh,
        in_specs=(
            P(None, ("rve", "slab"), None),
            P(None, ("rve", "slab"), None),
            P(None, ("rve", "slab"), None),
            P("rve", "slab", None),
            P("rve", "slab", None),
        ),
        out_specs=(P(None, ("rve", "slab"), None), P("rve", None, "slab", None), P()),
        check_vma=False,
    )
```

```python
import math

import jax
import jax.numpy as jnp
from jax import lax
from jax.experimental import pallas as pl
from jax.experimental.pallas import tpu as pltpu
from jax.sharding import PartitionSpec as P

MESH = pl.DeviceIdType.MESH
F32 = jnp.float32
BF16 = jnp.bfloat16

GRID = 256
HALF = 128
GROUPS = 32
SLABS = 8
BLOCK = 32
EXT = 48
CG_STEPS = 4

MU_REF = 2.0
LAMBDA_REF = 2.0
COUPLE = (LAMBDA_REF + MU_REF) / (MU_REF * (LAMBDA_REF + 2.0 * MU_REF))
LOWER = 0.5 - 0.5 / math.sqrt(3.0)
UPPER = 0.5 + 0.5 / math.sqrt(3.0)
ENDS = (LOWER, UPPER)
WEIGHT = 0.25
RANGE = 0.5

PAIRS = [(i, j) for i in range(CG_STEPS) for j in range(i, CG_STEPS + 1)]


def wave(slot, place):
    k = jnp.where(slot == HALF, HALF, lax.rem(slot, HALF))
    sine = slot > HALF
    turn = lax.bitwise_and(k * place + jnp.where(sine, 3 * GRID // 4, 0), GRID - 1)
    angle = (jnp.abs(turn - HALF) - GRID // 4).astype(F32) * (2.0 * math.pi / GRID)
    square = angle * angle
    value = 1.0 / 362880.0 - square * (1.0 / 39916800.0)
    for term in (1.0 / 5040.0, 1.0 / 120.0, 1.0 / 6.0, 1.0):
        value = term - square * value
    flat = (k == 0) | (k == HALF)
    return angle * value * jnp.where(flat, 1.0 / math.sqrt(GRID), math.sqrt(2.0 / GRID))


OFFSETS = sorted(
    ((dx, dz) for dx in range(4) for dz in range(8) if dx or dz),
    key=lambda o: -(min(o[0], 4 - o[0]) + min(o[1], 8 - o[1])),
)
NEAR = sorted(
    ((dy, dc) for dy in range(4) for dc in range(2) if dy or dc),
    key=lambda o: (-min(o[0], 4 - o[0]), -o[1]),
)


def lane_iota(shape):
    return lax.broadcasted_iota(jnp.int32, shape, len(shape) - 1)


def rows_up(field):
    rolled = pltpu.roll(field, field.shape[1] - 1, 1)
    return jnp.where(lane_iota(field.shape) == field.shape[1] - 1, 0.0, rolled)


def rows_down(field):
    rolled = pltpu.roll(field, 1, 1)
    return jnp.where(lane_iota(field.shape) == 0, 0.0, rolled)


def columns_back(field):
    return pltpu.roll(field, field.shape[0] - 1, 0)


def columns_on(field):
    return pltpu.roll(field, 1, 0)


def split(value):
    high = value.astype(BF16)
    return high, (value - high.astype(F32)).astype(BF16)


def dot(left, right):
    return jnp.dot(left, right, preferred_element_type=F32)


def strain_parts(first, second, first_next, second_next):
    slopes = []
    for here, beside in ((first, first_next), (second, second_next)):
        above = rows_up(here)
        both = rows_up(beside)
        across, across_up = beside - here, both - above
        up, up_next = above - here, both - beside
        slopes.append(
            (
                [(1.0 - t) * across + t * across_up for t in ENDS],
                [(1.0 - s) * up + s * up_next for s in ENDS],
            )
        )
    return slopes[0][0], slopes[1][1], slopes[0][1], slopes[1][0]


def strain_parts_ext(field):
    slopes = []
    for here in field:
        above = rows_up(here)
        beside, both = columns_back(here), columns_back(above)
        across, across_up = beside - here, both - above
        up, up_next = above - here, both - beside
        slopes.append(
            (
                [(1.0 - t) * across + t * across_up for t in ENDS],
                [(1.0 - s) * up + s * up_next for s in ENDS],
            )
        )
    return slopes[0][0], slopes[1][1], slopes[0][1], slopes[1][0]


def assemble(stress):
    by_t = lambda c, t: stress[2 * t][c] + stress[2 * t + 1][c]
    by_s = lambda c, s: stress[s][c] + stress[2 + s][c]

    def mixed(parts):
        low = sum(WEIGHT * (1.0 - ENDS[k]) * parts[k] for k in range(2))
        high = sum(WEIGHT * ENDS[k] * parts[k] for k in range(2))
        return low, high

    forces = []
    for normal_x, normal_y in ((0, 2), (2, 1)):
        low_x, high_x = mixed([by_t(normal_x, t) for t in range(2)])
        low_y, high_y = mixed([by_s(normal_y, s) for s in range(2)])
        on = low_x - high_y + rows_down(high_x + high_y)
        forces.append(columns_on(on) - (low_x + low_y) + rows_down(low_y - high_x))
    return forces


def inverse(value):
    guess = pl.reciprocal(value, approx=True)
    return guess * (2.0 - value * guess)


def law(strain, harden):
    volume = strain[0] + strain[1]
    normal = 0.5 * (strain[0] - strain[1])
    shear = 0.5 * strain[2]
    stiff = harden * (2.0 * normal * normal + 2.0 * shear * shear)
    factor = (1.0 + 2.0 * stiff) * inverse(1.0 + 3.0 * stiff)
    for turn in range(2):
        square = stiff * factor * factor
        factor = (1.0 + 2.0 * square * factor) * inverse(1.0 + 3.0 * square)
    square = factor * factor
    slope = -harden * square * factor * inverse(1.0 + 3.0 * stiff * square)
    return volume, normal, shear, factor, slope


def stress_of(state, bulk, modulus):
    volume, normal, shear, factor, slope = state
    spread = 2.0 * modulus * factor
    return [bulk * volume + spread * normal, bulk * volume - spread * normal, spread * shear]


def image_of(state, bulk, modulus, rest):
    volume, normal, shear, factor, slope = state
    d_volume = rest[0] + rest[1]
    d_normal = 0.5 * (rest[0] - rest[1])
    d_shear = 0.5 * rest[2]
    d_factor = slope * (4.0 * normal * d_normal + 4.0 * shear * d_shear)
    d_dev = 2.0 * modulus * (factor * d_normal + d_factor * normal)
    return [
        bulk * d_volume + d_dev,
        bulk * d_volume - d_dev,
        2.0 * modulus * (factor * d_shear + d_factor * shear),
    ]


def green(first, second, mixed, part_11, part_22, cross):
    across = cross * mixed
    one, two = part_11 * first + across, part_22 * second + across
    total = (2.0 * MU_REF * COUPLE / 2.0) * (one + two)
    return (
        one - part_11 * total,
        two - part_22 * total,
        cross * (first + second - 2.0 * total) + (part_11 + part_22) * mixed,
    )


def kernel(
    disp_hbm, body_hbm, assign_hbm, phase_hbm, flag_hbm,
    correction_out, strain_0, strain_1, strain_2, hom_out,
    disp, body, assign, table, pf, a1src, a1, nb, a2src, a2, c1src, c1, c2src, c2, d1src, d1, d2src, d2,
    halo_u, halo_f, halo_a,
    parts, labels, accs, green_tab, ph_f, hard_f, mid_h, mid_l, spec, filt_h, filt_l,
    strains, last, basis, tangent,
    relay, load, send, recv, gather_recv, halo_recv,
):
    r = lax.axis_index("rve")
    s = lax.axis_index("slab")
    y, core = s // 2, s % 2
    half, lane_field = s // 4, s % 4
    before, after = lax.rem(r + GROUPS - 1, GROUPS), lax.rem(r + 1, GROUPS)
    peers = [(r, lax.rem(y + dy, 4) * 2 + (1 - core if dc else core)) for dy, dc in NEAR]
    gx, gz = r // 8, r % 8
    far = [(lax.rem(gx + dx, 4) * 8 + lax.rem(gz + dz, 8), s) for dx, dz in OFFSETS]
    left = (jnp.where(s == 0, before, r), lax.rem(s + SLABS - 1, SLABS))
    right = (jnp.where(s == SLABS - 1, after, r), lax.rem(s + 1, SLABS))

    loads = [
        pltpu.make_async_copy(source, target, load.at[k])
        for k, (source, target) in enumerate(
            (
                (disp_hbm, disp),
                (assign_hbm, assign),
                (phase_hbm.at[0], pf.at[core, y, 0]),
                (flag_hbm.at[0], pf.at[core, y, 1]),
                (body_hbm, body),
            )
        )
    ]
    for copy in loads:
        copy.start()

    barrier = pltpu.get_barrier_semaphore()

    def greet(device):
        pl.semaphore_signal(barrier, inc=1, device_id=device, device_id_type=MESH)

    ring_z = {dz: (gx * 8 + lax.rem(gz + dz, 8), s) for dz in (1, 2, 6, 7)}
    ring_x = [(lax.rem(gx + dx, 4) * 8 + gz, s) for dx in (2, 1, 3)]
    opposite = y == 2
    across = (jnp.where(opposite, before, after), jnp.where(opposite, SLABS - 1, 0))
    has_across = jnp.where(opposite, r > 0, r < GROUPS - 1)
    gives_back, gives_on = (s == 0) & (r > 0), (s == SLABS - 1) & (r < GROUPS - 1)
    has_left, has_right = (s > 0) | (r > 0), (s < SLABS - 1) | (r < GROUPS - 1)

    @pl.when(has_across)
    def _():
        greet(across)

    @pl.when(gives_back)
    def _():
        for k in (0, 1, 2, 3, 6, 7):
            greet((before, k))

    @pl.when(gives_on)
    def _():
        for k in (4, 5):
            greet((after, k))

    for device in [ring_z[2], ring_z[6]] + ring_x + peers + [ring_z[1], ring_z[7]]:
        greet(device)

    def label_sums(rows, count):
        step = rows // 8

        def one(label, _):
            e = [parts[k, 0:rows, :] for k in range(8)]
            mask = [jnp.where(labels[p, 0:rows, :] == label.astype(F32), 1.0, 0.0) for p in range(4)]
            t_low, t_high = mask[0] + mask[1], mask[2] + mask[3]
            s_low, s_high = mask[0] + mask[2], mask[1] + mask[3]
            sums = [
                e[0] * t_low + e[1] * t_high,
                e[2] * s_low + e[3] * s_high,
                e[4] * s_low + e[5] * s_high + e[6] * t_low + e[7] * t_high,
            ]
            if count:
                sums.append(t_low + t_high)
            for c in range(len(sums)):
                accs[c, label] = jnp.sum(sums[c].reshape(step, 8, 128), axis=0)
            return 0

        lax.fori_loop(0, GROUPS, one, 0, unroll=GROUPS if rows == 8 else 4)
        used = 4 if count else 3
        folded = jnp.sum(accs[0:used].reshape(used * GROUPS, 8, 128), axis=1)
        if not count:
            folded = jnp.concatenate([folded, jnp.zeros((GROUPS, 128), F32)], axis=0)
        ones = jnp.ones((8, 128), BF16)
        total = jnp.zeros((8, 128), F32)
        for turn in range(3):
            piece = folded.astype(BF16)
            folded = folded - piece.astype(F32)
            total = total + lax.dot_general(
                ones, piece, (((1,), (1,)), ((), ())), preferred_element_type=F32
            )
        return total[0:1, :]

    def keep_parts(fields, rows):
        d1x, d2y, d1y, d2x = strain_parts(*fields)
        for k, value in enumerate(d1x + d2y + d1y + d2x):
            parts[k, 0:rows, :] = value

    row_of = lax.broadcasted_iota(jnp.int32, (BLOCK, 128), 0)
    loads[0].wait()
    loads[1].wait()
    own = [disp[0], disp[1]]
    beside = [jnp.where(row_of == BLOCK - 1, 0.0, columns_back(u)) for u in own]
    keep_parts(own + beside, BLOCK)
    for p in range(4):
        labels[p] = assign[p].astype(F32)
    a1src[...] = jnp.concatenate(
        [label_sums(BLOCK, True), disp[0, 0:1, :], disp[1, 0:1, :]]
        + [labels[p, BLOCK - 1 : BLOCK, :] for p in range(4)]
        + [jnp.zeros((1, 128), F32)],
        axis=0,
    )
    a1[s] = a1src[...]

    for copy in loads[2:5]:
        copy.wait()
    pl.semaphore_wait(
        barrier,
        SLABS - 1 + 3 + 4 + jnp.where(has_across, 1, 0) + jnp.where(gives_back, 6, 0) + jnp.where(gives_on, 2, 0),
    )

    def push(source, target, k, recv_sem, device):
        pltpu.make_async_remote_copy(
            source, target, send.at[k], recv_sem, device_id=device, device_id_type=MESH
        ).start()

    def drained(ref, sem):
        pltpu.make_async_copy(ref, ref, sem).wait()

    @pl.when(gives_back)
    def _():
        for k in (0, 1, 2, 3, 6, 7):
            push(a1src, nb, 1, recv.at[1], (before, k))

    @pl.when(gives_on)
    def _():
        for k in (4, 5):
            push(a1src, nb, 1, recv.at[1], (after, k))

    for device in peers:
        push(a1src, a1.at[s], 0, recv.at[0], device)

    strip = ((disp, halo_u), (body, halo_f), (assign, halo_a))

    def tell(k, devices):
        for device in devices:
            pl.semaphore_signal(relay.at[k], inc=1, device_id=device, device_id_type=MESH)

    tell(0, [ring_z[2], ring_z[6]])
    sibling = (r, y * 2 + 1 - core)
    for k in range(1, 4):
        push(pf.at[core, y], pf.at[core, y], 2, gather_recv.at[y], (r, lax.rem(y + k, 4) * 2 + core))
    push(pf.at[core, y], pf.at[core, y], 3, recv.at[2], sibling)

    def symbols(k, _):
        rows = pl.ds(pl.multiple_of(k * 32, 32), 32)
        row = lax.broadcasted_iota(jnp.int32, (32, GRID), 0) + k * 32
        lane = lax.broadcasted_iota(jnp.int32, (32, GRID), 1)
        k1 = lax.rem(row, HALF).astype(F32)
        k2 = lax.rem(lane, HALF).astype(F32)
        square = k1 * k1 + k2 * k2
        inverse = jnp.where(square > 0.0, 1.0 / jnp.maximum(square, 1.0), 0.0)
        sign = jnp.where((row < HALF) == (lane < HALF), -1.0, 1.0)
        green_tab[0, rows, :] = k1 * k1 * inverse
        green_tab[1, rows, :] = k2 * k2 * inverse
        green_tab[2, rows, :] = sign * k1 * k2 * inverse
        table[0, rows, :], table[1, rows, :] = split(wave(row, lane))
        table[2, rows, :], table[3, rows, :] = split(wave(lane, row))
        return 0

    lax.fori_loop(0, 8, symbols, 0)

    pl.semaphore_wait(relay.at[0], 2)
    tell(1, ring_x)

    drained(a1.at[pl.ds(0, SLABS - 1)], recv.at[0])
    @pl.when(has_across)
    def _():
        drained(nb, recv.at[1])

    @pl.when(jnp.logical_not(has_across))
    def _():
        nb[...] = jnp.zeros((8, 128), F32)

    row8 = lax.broadcasted_iota(jnp.int32, (8, 128), 0)
    gathered = a1[...]
    counted = jnp.where(has_across, 1.0, 0.0)
    nxt = []
    for c in range(2):
        own_c = jnp.concatenate([gathered[k, 1 + c : 2 + c, :] for k in range(SLABS)], axis=0)
        outer = jnp.where(opposite, gathered[0, 1 + c : 2 + c, :], nb[1 + c : 2 + c, :]) * counted
        nxt.append(jnp.where(row8 == 7, outer, columns_back(own_c)))
    zero8 = jnp.zeros((8, 128), F32)
    keep_parts([zero8, zero8] + nxt, 8)
    for p in range(4):
        outer = jnp.where(opposite, nb[3 + p : 4 + p, :], gathered[SLABS - 1, 3 + p : 4 + p, :])
        labels[p, 0:8, :] = jnp.concatenate(
            [gathered[k, 3 + p : 4 + p, :] for k in range(SLABS - 1)] + [outer], axis=0
        )
    a2src[...] = label_sums(8, False) + jnp.sum(gathered, axis=0)[0:1, :]
    a2[r] = a2src[...]
    pl.semaphore_wait(relay.at[1], 3)
    for device in far:
        push(a2src, a2.at[r], 10, recv.at[3], device)

    @pl.when(has_left)
    def _():
        for k, (own_ref, halo) in enumerate(strip):
            push(own_ref.at[:, pl.ds(0, 8), :], halo.at[1], 4 + 2 * k, halo_recv.at[k, 1], left)

    @pl.when(has_right)
    def _():
        for k, (own_ref, halo) in enumerate(strip):
            push(own_ref.at[:, pl.ds(BLOCK - 8, 8), :], halo.at[0], 5 + 2 * k, halo_recv.at[k, 0], right)

    def take_block(slab, chip):
        rows = pl.ds(pl.multiple_of((chip * 2 + slab) * BLOCK, BLOCK), BLOCK)
        here = pf[slab, chip, 0].astype(F32)
        active = pf[slab, chip, 1].astype(F32)
        ph_f[rows, :] = here
        hard_f[rows, :] = active * (2.0 - 1.5 * here)
        kinds_of = [here.astype(BF16), active.astype(BF16), (here * active).astype(BF16)]
        block = jnp.concatenate(kinds_of, axis=0)
        value = dot(block, table[2]) + dot(block, table[3])
        for m in range(3):
            part_h, part_l = split(value[m * BLOCK : (m + 1) * BLOCK])
            mid_h[m, rows, :] = part_h
            mid_l[m, rows, :] = part_l

    take_block(core, y)
    for k in range(1, 4):
        other = lax.rem(y + k, 4)
        drained(pf.at[core, other], gather_recv.at[other])
        push(pf.at[core, other], pf.at[core, other], 3, recv.at[2], sibling)
        take_block(core, other)
    drained(pf.at[1 - core], recv.at[2])
    for k in range(4):
        take_block(1 - core, k)

    def along_x(high, low, rows=slice(None), which=0):
        left_h, left_l = table[which, rows, :], table[which + 1, rows, :]
        return dot(left_h, high) + dot(left_h, low) + dot(left_l, high)

    def along_y(high, low, which):
        right_h, right_l = table[which], table[which + 1]
        return dot(high, right_h) + dot(high, right_l) + dot(low, right_h)

    for m in range(3):
        spec[m] = along_x(mid_h[m], mid_l[m])

    drained(a2.at[pl.ds(0, GROUPS - 1)], recv.at[3])
    totals = jnp.sum(a2[...], axis=0)
    lane1 = lane_iota((1, 128))
    picked = [
        jnp.sum(jnp.where(lane1 == 32 * c + r, totals, 0.0), axis=1, keepdims=True) for c in range(4)
    ]
    mean = [jnp.broadcast_to(picked[c] / picked[3], (8, 128)) for c in range(3)]
    unit = [jnp.where(lane_field == c, 1.0, 0.0) + jnp.where((lane_field == 3) & (c == 2), 1.0, 0.0) for c in range(3)]
    units = [jnp.full((8, 128), u, F32) for u in unit]

    kinds = {}
    for p in range(2):
        bulk, modulus = (6.0, 3.0) if p else (2.0, 1.0)
        for f in range(2):
            state = law(mean, (0.5 if p else 2.0) * f)
            kinds[p, f] = stress_of(state, bulk / MU_REF, modulus / MU_REF) + image_of(
                state, bulk / MU_REF, modulus / MU_REF, units
            )
    weights = []
    for k in range(6):
        base = kinds[0, 0][k]
        by_phase = kinds[1, 0][k] - base
        by_flag = kinds[0, 1][k] - base
        weights.append((by_phase, by_flag, kinds[1, 1][k] - base - by_phase - by_flag))

    def filter_pieces(load, n):
        def piece(k):
            for a in range(2):
                rows = slice(a * HALF + k * 16, a * HALF + k * 16 + 16)
                swap_rows = slice((1 - a) * HALF + k * 16, (1 - a) * HALF + k * 16 + 16)
                for b in range(2):
                    lanes = slice(b * HALF, (b + 1) * HALF)
                    swap_lanes = slice((1 - b) * HALF, (2 - b) * HALF)
                    sym = [green_tab[i, rows, lanes] for i in range(3)]
                    out = green(*load(n, rows, lanes, swap_rows, swap_lanes), *sym)
                    for c in range(3):
                        rr, ll = (swap_rows, swap_lanes) if c == 2 else (rows, lanes)
                        high, low = split(out[c])
                        filt_h[3 * n + c, rr, ll] = high
                        filt_l[3 * n + c, rr, ll] = low

        return [lambda k=k: piece(k) for k in range(8)]

    def together(first, second):
        turns = max(len(first), len(second))
        for k in range(turns):
            for pieces in (first, second):
                for j in range(k * len(pieces) // turns, (k + 1) * len(pieces) // turns):
                    pieces[j]()

    def wide(value):
        return jnp.concatenate([value, value], axis=0)

    wide_weights = [[wide(w) for w in three] for three in weights]

    def load_first(n, rows, lanes, swap_rows, swap_lanes):
        here = [spec[m, rows, lanes] for m in range(3)]
        there = [spec[m, swap_rows, swap_lanes] for m in range(3)]
        mix = lambda k, fields: sum(wide_weights[k][m] * fields[m] for m in range(3))
        return mix(3 * n, here), mix(3 * n + 1, here), mix(3 * n + 2, there)

    start = mean + units

    def invert_first(n):
        def one(k):
            high, low = split(along_x(filt_h[k], filt_l[k], which=2))
            strains[k] = jnp.broadcast_to(start[k][0:1, 0:1], (GRID, GRID)) - along_y(high, low, 0)

        return [lambda k=k: one(k) for k in range(3 * n, 3 * n + 3)]

    for piece in filter_pieces(load_first, 0):
        piece()
    together(filter_pieces(load_first, 1), invert_first(0))
    for piece in invert_first(1):
        piece()

    def material(k):
        rows = slice(k * 16, k * 16 + 16)
        for b in range(2):
            lanes = slice(b * HALF, (b + 1) * HALF)
            here = ph_f[rows, lanes]
            state = law([strains[c, rows, lanes] for c in range(3)], hard_f[rows, lanes])
            bulk, modulus = 1.0 + 2.0 * here, 0.5 + here
            values = stress_of(state, bulk, modulus) + image_of(
                state, bulk, modulus, [strains[3 + c, rows, lanes] for c in range(3)]
            )
            for c in range(6):
                filt_h[c, rows, lanes], filt_l[c, rows, lanes] = split(values[c])

    def forward_y(q):
        rows = slice(q * 64, q * 64 + 64)
        stacked = lambda ref: jnp.concatenate([ref[c, rows, :] for c in range(6)], axis=0)
        high, low = split(along_y(stacked(filt_h), stacked(filt_l), 2))
        for c in range(6):
            mid_h[c, rows, :] = high[c * 64 : c * 64 + 64]
            mid_l[c, rows, :] = low[c * 64 : c * 64 + 64]

    for q in range(5):
        pieces = [lambda k=k: material(k) for k in range(4 * q, 4 * q + 4)] if q < 4 else []
        together(pieces, [lambda: forward_y(q - 1)] if q else [])

    def load_second(n, rows, lanes, swap_rows, swap_lanes):
        return spec[3 * n, rows, lanes], spec[3 * n + 1, rows, lanes], spec[3 * n + 2, swap_rows, swap_lanes]

    part = pl.ds(pl.multiple_of(half * HALF, HALF), HALF)

    def forward_x(n):
        def one(k):
            spec[k] = along_x(mid_h[k], mid_l[k])

        return [lambda k=k: one(k) for k in range(3 * n, 3 * n + 3)]

    def invert_second(n):
        def one(k):
            high, low = split(along_x(filt_h[k], filt_l[k], rows=part, which=2))
            last[k] = strains[k, part, :] - along_y(high, low, 0)

        return [lambda k=k: one(k) for k in range(3 * n, 3 * n + 3)]

    for piece in forward_x(0):
        piece()
    together(filter_pieces(load_second, 0), forward_x(1))
    together(filter_pieces(load_second, 1), invert_second(0))
    for piece in invert_second(1):
        piece()

    def finish(k, sums):
        rows = pl.ds(pl.multiple_of(k * 16, 16), 16)
        full = pl.ds(pl.multiple_of(half * HALF + k * 16, 16), 16)
        sums = list(sums)
        for b in range(2):
            lanes = slice(b * HALF, (b + 1) * HALF)
            here = ph_f[full, lanes]
            state = law([last[c, rows, lanes] for c in range(3)], hard_f[full, lanes])
            bulk, modulus = 2.0 + 4.0 * here, 1.0 + 2.0 * here
            values = stress_of(state, bulk, modulus) + image_of(
                state, bulk, modulus, [last[3 + c, rows, lanes] for c in range(3)]
            )
            for c in range(6):
                sums[c] = sums[c] + values[c][0:8, :] + values[c][8:16, :]
        return tuple(sums)

    sums = lax.fori_loop(0, 8, finish, tuple(jnp.zeros((8, 128), F32) for c in range(6)), unroll=4)
    for c, strain_out in enumerate((strain_0, strain_1, strain_2)):
        strain_out[...] = last[c, pl.ds(pl.multiple_of(lane_field * BLOCK, BLOCK), BLOCK), :]

    message = jnp.zeros((1, 128), F32)
    for c in range(3):
        stress_sum, image_sum = [
            jnp.sum(jnp.sum(sums[k], axis=0, keepdims=True), axis=1, keepdims=True) * (1.0 / (GRID * GRID))
            for k in (c, 3 + c)
        ]
        message = message + jnp.where((lane1 == c) & (lane_field == 0), stress_sum, 0.0)
        message = message + jnp.where((lane1 == 3 + 3 * lane_field + c) & (lane_field < 3), image_sum, 0.0)
        message = message + jnp.where((lane1 == 12 + c) & (s == 0), mean[c][0:1, :], 0.0)
    c1src[...] = message
    c1[s] = message
    for device in peers:
        push(c1src, c1.at[s], 11, recv.at[4], device)

    for side, has_side in enumerate((has_left, has_right)):

        @pl.when(has_side)
        def _():
            for k, (own_ref, halo) in enumerate(strip):
                drained(halo.at[side], halo_recv.at[k, side])

        @pl.when(jnp.logical_not(has_side))
        def _():
            for own_ref, halo in strip:
                halo[side] = jnp.zeros(halo.shape[1:], halo.dtype)

    column = lax.broadcasted_iota(jnp.int32, (EXT, 128), 0) + ((r * SLABS + s) * BLOCK - 8)
    inside = (column >= 0) & (column < GROUPS * SLABS * BLOCK)

    def extended(halo, own_ref, c):
        return jnp.concatenate([halo[0, c], own_ref[c], halo[1, c]], axis=0)

    u = [jnp.where(inside, extended(halo_u, disp, c), 0.0) for c in range(2)]
    force = [extended(halo_f, body, c) for c in range(2)]
    index = [jnp.where(inside, extended(halo_a, assign, p), 127) for p in range(4)]
    u_parts = strain_parts_ext(u)

    drained(c1.at[pl.ds(0, SLABS - 1)], recv.at[4])
    c2src[...] = jnp.sum(c1[...], axis=0)
    c2[r] = c2src[...]
    for device in far:
        push(c2src, c2.at[r], 12, recv.at[5], device)
    drained(c2.at[pl.ds(0, GROUPS - 1)], recv.at[5])
    square = jnp.concatenate([c2[...].reshape(GROUPS, 128), jnp.zeros((128 - GROUPS, 128), F32)], axis=0)
    by_label = square.T[0:16, :]
    hom_out[...] = by_label[0:12, 0:GROUPS]
    rows = [by_label[k : k + 1, :] for k in range(15)]
    offset = [rows[c] - sum(rows[3 + 3 * j + c] * rows[12 + j] for j in range(3)) for c in range(3)]
    size = sum(jnp.abs(rows[k]) for k in range(3, 12))
    scale = RANGE * jnp.max(size, axis=1, keepdims=True)
    inverse_scale = 1.0 / scale

    def looked(row, p):
        return jnp.take_along_axis(jnp.broadcast_to(row, (EXT, 128)), index[p], axis=1, mode="promise_in_bounds")

    def point_strain(shapes, p):
        d1x, d2y, d1y, d2x = shapes
        sp, tp = p % 2, p // 2
        return d1x[tp], d2y[sp], d1y[sp] + d2x[tp]

    stress = []
    for p in range(4):
        strain = point_strain(u_parts, p)
        cs = [looked(rows[3 + k], p) for k in range(9)]
        for k in range(9):
            tangent[p, k] = cs[k]
        stress.append(
            [
                looked(offset[c], p) + cs[c] * strain[0] + cs[3 + c] * strain[1] + cs[6 + c] * strain[2]
                for c in range(3)
            ]
        )
    forces = assemble(stress)
    vector = [jnp.where(inside, force[c] - forces[c], 0.0) for c in range(2)]
    history = [vector]
    basis[0, 0], basis[0, 1] = vector[0][8:40], vector[1][8:40]

    def stiffness(field):
        shapes = strain_parts_ext(field)
        result = []
        for p in range(4):
            strain = point_strain(shapes, p)
            result.append(
                [
                    tangent[p, c] * strain[0] + tangent[p, 3 + c] * strain[1] + tangent[p, 6 + c] * strain[2]
                    for c in range(3)
                ]
            )
        return assemble(result)

    for k in range(CG_STEPS):
        image = stiffness(history[k])
        shifted = [jnp.where(inside, image[c] * inverse_scale - history[k][c], 0.0) for c in range(2)]
        if k:
            shifted = [2.0 * shifted[c] - history[k - 1][c] for c in range(2)]
        history.append(shifted)
        basis[k + 1, 0], basis[k + 1, 1] = shifted[0][8:40], shifted[1][8:40]

    dots = []
    for i, j in PAIRS:
        product = basis[i, 0] * basis[j, 0] + basis[i, 1] * basis[j, 1]
        dots.append(jnp.sum(product.reshape(4, 8, 128), axis=(0, 1), keepdims=True).reshape(1, 128))
    dots += [jnp.zeros((1, 128), F32)] * (16 - len(dots))
    stacked = jnp.sum(jnp.concatenate(dots, axis=0), axis=1, keepdims=True)
    diagonal = lax.broadcasted_iota(jnp.int32, (16, 128), 0) == lane_iota((16, 128))
    d1src[...] = jnp.sum(jnp.where(diagonal, stacked, 0.0), axis=0, keepdims=True)
    d1[s] = d1src[...]
    for device in peers:
        push(d1src, d1.at[s], 13, recv.at[6], device)
    drained(d1.at[pl.ds(0, SLABS - 1)], recv.at[6])
    d2src[...] = jnp.sum(d1[...], axis=0)
    d2[r] = d2src[...]
    for device in far:
        push(d2src, d2.at[r], 14, recv.at[7], device)
    drained(d2.at[pl.ds(0, GROUPS - 1)], recv.at[7])
    gram_row = jnp.sum(d2[...], axis=0)
    gram = {}
    for k, (i, j) in enumerate(PAIRS):
        value = jnp.sum(jnp.where(lane1 == k, gram_row, 0.0), axis=1, keepdims=True)
        gram[i, j] = gram[j, i] = value

    def inner(one, two):
        return sum(one[i] * two[j] * gram[i, j] for i in range(len(one)) for j in range(len(two)))

    def apply(coefficients):
        n = len(coefficients)
        result = [scale * c for c in coefficients] + [0.0]
        for k in range(n):
            if k == 0:
                result[1] = result[1] + scale * coefficients[0]
            else:
                result[k + 1] = result[k + 1] + 0.5 * scale * coefficients[k]
                result[k - 1] = result[k - 1] + 0.5 * scale * coefficients[k]
        return result

    one = jnp.ones((1, 1), F32)
    direction, residual = [one], [one]
    answer = []
    rho = gram[0, 0]
    for step in range(CG_STEPS):
        image = apply(direction)
        alpha = rho / inner(direction, image)
        answer = [
            (answer[k] if k < len(answer) else 0.0) + alpha * direction[k] for k in range(len(direction))
        ]
        if step == CG_STEPS - 1:
            break
        residual = [
            (residual[k] if k < len(residual) else 0.0) - alpha * image[k] for k in range(len(image))
        ]
        fresh = inner(residual, residual)
        beta = fresh / rho
        direction = [
            residual[k] + (beta * direction[k] if k < len(direction) else 0.0) for k in range(len(residual))
        ]
        rho = fresh
    for c in range(2):
        correction_out[c] = sum(answer[k] * basis[k, c] for k in range(CG_STEPS))

    drained(a1.at[pl.ds(0, SLABS - 1)], send.at[0])

    @pl.when(gives_back)
    def _():
        drained(a1.at[pl.ds(0, 6)], send.at[1])

    @pl.when(gives_on)
    def _():
        drained(a1.at[pl.ds(0, 2)], send.at[1])

    drained(pf.at[0, pl.ds(0, 3)], send.at[2])
    drained(pf.at[0], send.at[3])
    for side, has_side in enumerate((has_left, has_right)):

        @pl.when(has_side)
        def _():
            for k, (own_ref, halo) in enumerate(strip):
                drained(halo.at[side], send.at[4 + 2 * k + side])

    drained(a2.at[pl.ds(0, GROUPS - 1)], send.at[10])
    drained(c1.at[pl.ds(0, SLABS - 1)], send.at[11])
    drained(c2.at[pl.ds(0, GROUPS - 1)], send.at[12])
    drained(d1.at[pl.ds(0, SLABS - 1)], send.at[13])
    drained(d2.at[pl.ds(0, GROUPS - 1)], send.at[14])


def write_kernel(one, two_a, two_b, two_c, three, one_out, two_out, three_out, sems):
    copies = [
        pltpu.make_async_copy(source, target, sems.at[k])
        for k, (source, target) in enumerate(
            (
                (one, one_out),
                (two_a, two_out.at[0, 0]),
                (two_b, two_out.at[0, 1]),
                (two_c, two_out.at[0, 2]),
                (three, three_out),
            )
        )
    ]
    for copy in copies:
        copy.start()
    for copy in copies:
        copy.wait()


def written(*values):
    return pl.pallas_call(
        write_kernel,
        out_shape=(
            jax.ShapeDtypeStruct((2, BLOCK, 128), F32),
            jax.ShapeDtypeStruct((1, 3, BLOCK, GRID), F32),
            jax.ShapeDtypeStruct((12, GROUPS), F32),
        ),
        in_specs=[pl.BlockSpec(memory_space=pl.ANY)] * 5,
        out_specs=(pl.BlockSpec(memory_space=pltpu.HBM),) * 3,
        scratch_shapes=[pltpu.SemaphoreType.DMA((5,))],
        compiler_params=pltpu.CompilerParams(vmem_limit_bytes=4 * 1024 * 1024),
        name="write_out",
    )(*values)


def shards(displacement, body_force, assignment, phases, flags):
    vmem = pl.BlockSpec(memory_space=pltpu.VMEM)
    row = lambda n: pltpu.VMEM((n, 1, 128), F32)
    one_row = pltpu.VMEM((1, 128), F32)
    square = (GRID, GRID)
    results = pl.pallas_call(
        kernel,
        out_shape=(
            jax.ShapeDtypeStruct((2, BLOCK, 128), F32),
            jax.ShapeDtypeStruct((BLOCK, GRID), F32),
            jax.ShapeDtypeStruct((BLOCK, GRID), F32),
            jax.ShapeDtypeStruct((BLOCK, GRID), F32),
            jax.ShapeDtypeStruct((12, GROUPS), F32),
        ),
        in_specs=[pl.BlockSpec(memory_space=pltpu.HBM)] * 5,
        out_specs=(vmem,) * 5,
        scratch_shapes=[
            pltpu.VMEM((2, BLOCK, 128), F32),
            pltpu.VMEM((2, BLOCK, 128), F32),
            pltpu.VMEM((4, BLOCK, 128), jnp.int32),
            pltpu.VMEM((4,) + square, BF16),
            pltpu.VMEM((2, 4, 2, BLOCK, GRID), jnp.int32),
            pltpu.VMEM((8, 128), F32),
            pltpu.VMEM((SLABS, 8, 128), F32),
            pltpu.VMEM((8, 128), F32),
            one_row, row(GROUPS), one_row, row(SLABS), one_row, row(GROUPS),
            one_row, row(SLABS), one_row, row(GROUPS),
            pltpu.VMEM((2, 2, 8, 128), F32),
            pltpu.VMEM((2, 2, 8, 128), F32),
            pltpu.VMEM((2, 4, 8, 128), jnp.int32),
            pltpu.VMEM((8, BLOCK, 128), F32),
            pltpu.VMEM((4, BLOCK, 128), F32),
            pltpu.VMEM((4, GROUPS, 8, 128), F32),
            pltpu.VMEM((3,) + square, F32),
            pltpu.VMEM(square, F32),
            pltpu.VMEM(square, F32),
            pltpu.VMEM((6,) + square, BF16),
            pltpu.VMEM((6,) + square, BF16),
            pltpu.VMEM((6,) + square, F32),
            pltpu.VMEM((6,) + square, BF16),
            pltpu.VMEM((6,) + square, BF16),
            pltpu.VMEM((6,) + square, F32),
            pltpu.VMEM((6, HALF, GRID), F32),
            pltpu.VMEM((CG_STEPS + 1, 2, BLOCK, 128), F32),
            pltpu.VMEM((4, 9, EXT, 128), F32),
            pltpu.SemaphoreType.REGULAR((2,)),
            pltpu.SemaphoreType.DMA((5,)),
            pltpu.SemaphoreType.DMA((15,)),
            pltpu.SemaphoreType.DMA((8,)),
            pltpu.SemaphoreType.DMA((4,)),
            pltpu.SemaphoreType.DMA((3, 2)),
        ],
        compiler_params=pltpu.CompilerParams(
            collective_id=0, has_side_effects=True, vmem_limit_bytes=55080 * 1024
        ),
        name="fe2_step",
    )(displacement, body_force, assignment, phases, flags)
    return written(*results)


def solution(mesh):
    return jax.shard_map(
        shards,
        mesh=mesh,
        in_specs=(
            P(None, ("rve", "slab"), None),
            P(None, ("rve", "slab"), None),
            P(None, ("rve", "slab"), None),
            P("rve", "slab", None),
            P("rve", "slab", None),
        ),
        out_specs=(P(None, ("rve", "slab"), None), P("rve", None, "slab", None), P()),
        check_vma=False,
    )
```
